256 devices in a mesh: fsdp: 8 (over z_lo, core), seq: 8 (over y, z_hi), dp: 4 (over x).
Axes of the slice: x: 4, y: 4, z: 8 (z_hi: 2, z_lo: 4; z = z_hi * 4 + z_lo), core: 2. Of those that a mesh axis runs over, the one named last changes fastest.
Arguments:
- hidden: bfloat16 [32, 2, 512, 2048], P(('fsdp', 'dp'), None, 'seq'), may hold values from -3 to 3
- answer_rows: bfloat16 [32, 2, 512, 2048], P(('fsdp', 'dp'), None, 'seq'), may hold values from -0.125 to 0.125
- resp_mask: int32 [32, 2, 512], P(('fsdp', 'dp'), None, 'seq'), may hold values from 0 to 1, as said below
- attn_gain: float32 [2048], replicated, may hold values from 0.5 to 1.5
- final_gain: float32 [2048], replicated, may hold values from 0.5 to 1.5
- w_query: bfloat16 [2048, 2048], P(('fsdp', 'dp'))
- w_key: bfloat16 [2048, 512], P(('fsdp', 'dp'))
- w_value: bfloat16 [2048, 512], P(('fsdp', 'dp')), may hold values from -0.125 to 0.125
- w_out: bfloat16 [2048, 2048], P(('fsdp', 'dp')), may hold values from -0.125 to 0.125
- a_query: bfloat16 [2048, 64], P(('fsdp', 'dp')), may hold values from -0.125 to 0.125
- b_query: bfloat16 [2048, 64], P(('fsdp', 'dp')), may hold values from -0.375 to 0.375
- a_value: bfloat16 [2048, 64], P(('fsdp', 'dp')), may hold values from -0.125 to 0.125
- b_value: bfloat16 [512, 64], P(('fsdp', 'dp')), may hold values from -0.375 to 0.375
Outputs:
- grad_a_query: float32 [2048, 64], P(('fsdp', 'dp'))
- grad_b_query: float32 [2048, 64], P(('fsdp', 'dp'))
- grad_a_value: float32 [2048, 64], P(('fsdp', 'dp'))
- grad_b_value: float32 [512, 64], P(('fsdp', 'dp'))
- dpo_loss: float32 [32], P(('fsdp', 'dp'))
The draws below stay inside these ranges and needn't reach their ends.
Inputs may be any that keep to these rules, and one draw needn't show every extreme that they name: `resp_mask`: each sequence is 0 on a prompt of 64 to 256 positions and 1 on every later position; both sequences of a pair have the same prompt length.
All inputs are finite; a program needn't handle non-finite values.
Results may differ from the reference program's by a relative error of at most 0.029.
The reference program's roundings to bfloat16 on the way count: a program that leaves them out, or rounds other values in their place, can miss the bound.
Values may be sent and summed in bfloat16 or wider, within the bound.
No kernel may reach another device: no remote copies, remote signals or barrier semaphores. Data moves between devices by JAX's collectives and lax.ppermute only.
A program may use at most 64 MiB of HBM per device.

```python
import math
import jax
import jax.numpy as jnp
from jax import lax

D = 2048
HQ = 16
HK = 4
HD = 128
RANK = 64
TOK_DEV = 64
L = 512
PAIRS = 32
N_SEQ = 8


def query_base(key):
    return jnp.clip(jax.random.normal(key, (D, HQ * HD), jnp.float32), -4.0, 4.0)


def draw_w_query(key, part):
    return (query_base(key) * D ** (-0.5)).astype(jnp.bfloat16)


def draw_w_key(key, part):
    key = jax.random.fold_in(key, 23)
    own_part = jnp.clip(jax.random.normal(key, (D, HK * HD), jnp.float32), -4.0, 4.0)
    return (own_part * D ** (-0.5)).astype(jnp.bfloat16)


def draw_hidden(key, part):
    key = jax.random.fold_in(key, 31)
    return jnp.clip(0.6 * jax.random.normal(key, (PAIRS, 2, L, D), jnp.float32), -3.0, 3.0).astype(jnp.bfloat16)


def draw_resp_mask(key, part):
    key = jax.random.fold_in(key, 11)
    prompt = jax.random.randint(key, (PAIRS, 1, 1), L // 8, L // 2 + 1)
    where_pos = jnp.arange(L, dtype=jnp.int32)[None, None, :]
    return jnp.broadcast_to(where_pos >= prompt, (PAIRS, 2, L)).astype(jnp.int32)


def steps_of(own_key, shape, cuts, least, largest):
    level, own = 1.0, jax.random.fold_in(own_key, 6)
    for dim, parts in cuts:
        draws = jnp.exp(jax.random.uniform(jax.random.fold_in(own, dim), (parts,), jnp.float32, least / len(cuts), largest / len(cuts)))
        level = level * jnp.repeat(draws, shape[dim] // parts).reshape([-1 if axis == dim else 1 for axis in range(len(shape))])
    return level


def noise(own_key, dims, width, limit, cuts=(), kind=jnp.bfloat16):
    drawn = jax.random.normal(own_key, dims, jnp.float32) * width
    if len(cuts) > 0:
        drawn = steps_of(own_key, dims, cuts, -0.22, 0.18) * drawn
    return jnp.clip(drawn, min=-limit, max=limit).astype(kind)


def setup_inputs(seed: int = 0) -> dict:
    seeds = jax.random.split(jax.random.key(seed), 14)
    return {
        "hidden": draw_hidden(jax.random.fold_in(seeds[13], 71), 0),
        "answer_rows": noise(seeds[1], (PAIRS, 2, L, D), D ** -0.5, 0.125, ((0, 32), (2, 8))),
        "resp_mask": draw_resp_mask(jax.random.fold_in(seeds[13], 71), 0),
        "attn_gain": jnp.clip(1.0 + 0.1 * jax.random.normal(seeds[3], (D,), jnp.float32), 0.5, 1.5),
        "final_gain": jnp.clip(1.0 + 0.1 * jax.random.normal(seeds[4], (D,), jnp.float32), 0.5, 1.5),
        "w_query": draw_w_query(jax.random.fold_in(seeds[13], 71), 0),
        "w_key": draw_w_key(jax.random.fold_in(seeds[13], 71), 0),
        "w_value": noise(seeds[7], (D, HK * HD), D ** -0.5, 0.125, ((0, 32),)),
        "w_out": noise(seeds[8], (HQ * HD, D), (HQ * HD) ** -0.5, 0.125, ((0, 32),)),
        "a_query": noise(seeds[9], (D, RANK), D ** -0.5, 0.125, ((0, 32),)),
        "b_query": noise(seeds[10], (HQ * HD, RANK), (4 * RANK) ** -0.5, 0.375, ((0, 32),)),
        "a_value": noise(seeds[11], (D, RANK), D ** -0.5, 0.125, ((0, 32),)),
        "b_value": noise(seeds[12], (HK * HD, RANK), (4 * RANK) ** -0.5, 0.375, ((0, 32),)),
    }


EPS = 1e-05
BETA = 0.1
ADAPTER_SCALE = 2.0
THETA = 500000.0

def norm_rows(values, gain):
    return values * lax.rsqrt(lax.optimization_barrier(jnp.mean(values * values, axis=-1, keepdims=True)) + EPS) * gain

def rotary_tables(positions, half_dim):
    frequency = THETA ** (-(jnp.arange(half_dim, dtype=jnp.float32) * 2.0) / (2.0 * half_dim))
    angles = positions.astype(jnp.float32)[:, None] * frequency[None, :]
    return (jnp.cos(angles), jnp.sin(angles))

def apply_rotary(values, cosine_lookup, sine_lookup, direction):
    half_dim = values.shape[-1] // 2
    lower_half = values[..., :half_dim]
    upper_half = values[..., half_dim:]
    cosine = cosine_lookup[:, None, :]
    sine_part = direction * sine_lookup[:, None, :]
    return jnp.concatenate([lower_half * cosine - upper_half * sine_part, upper_half * cosine + lower_half * sine_part], axis=-1)

def attend(queries, keys_all, values_all, allowed):
    group_size = HQ // HK
    grouped = queries.reshape(2, L, HK, group_size, HD).astype(jnp.float32)
    logits = jnp.einsum('sqkgd,spkd->skgqp', grouped, keys_all.astype(jnp.float32)) / math.sqrt(HD)
    logits = jnp.where(allowed, logits, -1e+30)
    row_peak = lax.optimization_barrier(jnp.max(logits, axis=-1, keepdims=True))
    raised = jnp.exp(logits - row_peak)
    softmax = raised / lax.optimization_barrier(jnp.sum(raised, axis=-1, keepdims=True))
    rounded = softmax.astype(jnp.bfloat16)
    mixed = jnp.einsum('skgqp,spkd->sqkgd', rounded.astype(jnp.float32), values_all.astype(jnp.float32))
    return (softmax, rounded, mixed)

def pair_terms(weights, hidden_pair, answer_pair, mask_pair):
    attn_gain, final_gain, w_query, w_key, w_value, w_out, a_query, b_query, a_value, b_value = weights
    row_count = 2 * L
    group_size = HQ // HK
    x_float = hidden_pair.astype(jnp.float32)
    normed = norm_rows(x_float, attn_gain).astype(jnp.bfloat16)
    flattened_rows = normed.reshape(row_count, D)
    query_frozen_weight = jnp.dot(flattened_rows, w_query, preferred_element_type=jnp.float32)
    base_k = jnp.dot(flattened_rows, w_key, preferred_element_type=jnp.float32)
    base_v = jnp.dot(flattened_rows, w_value, preferred_element_type=jnp.float32)
    query_reduced_rows = jnp.dot(flattened_rows, a_query, preferred_element_type=jnp.float32).astype(jnp.bfloat16)
    value_reduced_rows = jnp.dot(flattened_rows, a_value, preferred_element_type=jnp.float32).astype(jnp.bfloat16)
    positions = jnp.arange(L, dtype=jnp.int32)
    cosine_lookup, sine_lookup = rotary_tables(positions, HD // 2)
    query_shape_tuple = (2, L, HQ, HD)
    shape_kv = (2, L, HK, HD)
    query_ref = apply_rotary(query_frozen_weight.reshape(query_shape_tuple), cosine_lookup, sine_lookup, 1.0).astype(jnp.bfloat16)
    query_lift_factor = jnp.dot(query_reduced_rows, b_query.T, preferred_element_type=jnp.float32)
    policy_query_rows = apply_rotary((query_frozen_weight + ADAPTER_SCALE * query_lift_factor).reshape(query_shape_tuple), cosine_lookup, sine_lookup, 1.0).astype(jnp.bfloat16)
    keys_all = apply_rotary(base_k.reshape(shape_kv), cosine_lookup, sine_lookup, 1.0).astype(jnp.bfloat16)
    reference_value_rows = base_v.astype(jnp.bfloat16).reshape(shape_kv)
    value_lift_factor = jnp.dot(value_reduced_rows, b_value.T, preferred_element_type=jnp.float32).reshape(shape_kv)
    policy_value_rows = (lax.optimization_barrier(reference_value_rows).astype(jnp.float32) + ADAPTER_SCALE * value_lift_factor).astype(jnp.bfloat16)
    allowed = positions[:, None] >= positions[None, :]
    softmax_ref, rounded_ref, mixed_ref = attend(query_ref, keys_all, reference_value_rows, allowed)
    softmax_pol, rounded_pol, mixed_pol = attend(policy_query_rows, keys_all, policy_value_rows, allowed)
    answers = answer_pair.reshape(row_count, D).astype(jnp.float32)
    response = mask_pair.astype(jnp.float32)

    def readout(mixed):
        heads_out = mixed.astype(jnp.bfloat16).reshape(row_count, HQ * HD)
        residual = x_float.reshape(row_count, D) + jnp.dot(heads_out, w_out, preferred_element_type=jnp.float32)
        inverse = lax.rsqrt(lax.optimization_barrier(jnp.mean(residual * residual, axis=-1, keepdims=True)) + EPS)
        unit_rows = residual * inverse
        score = lax.optimization_barrier(jnp.sum(unit_rows * final_gain * answers, axis=-1)).reshape(2, L)
        return (inverse, unit_rows, lax.optimization_barrier(jnp.sum(response * score, axis=-1)))
    inverse_ref, unit_ref, total_ref = readout(mixed_ref)
    inverse_pol, unit_pol, total_pol = readout(mixed_pol)
    margin = total_pol[0] - total_ref[0] - (total_pol[1] - total_ref[1])
    loss = jax.nn.softplus(-BETA * margin)
    weight = -BETA * jax.nn.sigmoid(-BETA * margin)
    side_sign = jnp.array([1.0, -1.0], dtype=jnp.float32)
    pair_coeff = (weight * side_sign)[:, None] * response
    back_final = pair_coeff.reshape(row_count)[:, None] * final_gain * answers
    back_resid = inverse_pol * (back_final - unit_pol * lax.optimization_barrier(jnp.mean(back_final * unit_pol, axis=-1, keepdims=True)))
    back_rounded = back_resid.astype(jnp.bfloat16)
    back_heads = jnp.dot(back_rounded, w_out.T, preferred_element_type=jnp.float32).astype(jnp.bfloat16)
    back_heads = back_heads.reshape(2, L, HK, group_size, HD)
    row_dots = jnp.moveaxis(lax.optimization_barrier(jnp.sum(back_heads.astype(jnp.float32) * mixed_pol, axis=-1)), 1, -1)
    back_probs = jnp.einsum('sqkgd,spkd->skgqp', back_heads.astype(jnp.float32), policy_value_rows.astype(jnp.float32))
    back_logits = (softmax_pol * (back_probs - row_dots[..., None]) / math.sqrt(HD)).astype(jnp.bfloat16)
    back_query = jnp.einsum('skgqp,spkd->sqkgd', back_logits.astype(jnp.float32), keys_all.astype(jnp.float32))
    query_gradient_rows = apply_rotary(back_query.reshape(query_shape_tuple), cosine_lookup, sine_lookup, -1.0).astype(jnp.bfloat16).reshape(row_count, HQ * HD)
    prob_blocks = rounded_pol.reshape(2, HK, group_size, N_SEQ, TOK_DEV, L).astype(jnp.float32)
    heads_split = back_heads.reshape(2, N_SEQ, TOK_DEV, HK, group_size, HD).astype(jnp.float32)
    partial_value = jnp.einsum('skgcqp,scqkgd->cspkd', prob_blocks, heads_split)
    rounded_parts = lax.optimization_barrier(partial_value.astype(jnp.bfloat16)).astype(jnp.float32)
    value_gradient_rows = lax.optimization_barrier(jnp.sum(rounded_parts, axis=0)).astype(jnp.bfloat16).reshape(row_count, HK * HD)
    query_down_factor = jnp.dot(query_gradient_rows, b_query, preferred_element_type=jnp.float32).astype(jnp.bfloat16)
    value_down_factor = jnp.dot(value_gradient_rows, b_value, preferred_element_type=jnp.float32).astype(jnp.bfloat16)
    query_down_gradient = ADAPTER_SCALE * jnp.dot(flattened_rows.T, query_down_factor, preferred_element_type=jnp.float32)
    query_lift_gradient = ADAPTER_SCALE * jnp.dot(query_gradient_rows.T, query_reduced_rows, preferred_element_type=jnp.float32)
    value_down_gradient = ADAPTER_SCALE * jnp.dot(flattened_rows.T, value_down_factor, preferred_element_type=jnp.float32)
    value_lift_gradient = ADAPTER_SCALE * jnp.dot(value_gradient_rows.T, value_reduced_rows, preferred_element_type=jnp.float32)
    return ((query_down_gradient, query_lift_gradient, value_down_gradient, value_lift_gradient), loss)

def reference(hidden, answer_rows, resp_mask, attn_gain, final_gain, w_query, w_key, w_value, w_out, a_query, b_query, a_value, b_value):
    weights = (attn_gain, final_gain, w_query, w_key, w_value, w_out, a_query, b_query, a_value, b_value)

    def step(running, inputs):
        grads, loss = pair_terms(weights, inputs[0], inputs[1], inputs[2])
        return (tuple((total + extra for total, extra in zip(running, grads))), loss)
    initial = (jnp.zeros((D, RANK), jnp.float32), jnp.zeros((HQ * HD, RANK), jnp.float32), jnp.zeros((D, RANK), jnp.float32), jnp.zeros((HK * HD, RANK), jnp.float32))
    running, losses = lax.scan(step, initial, (hidden, answer_rows, resp_mask))
    return (running[0], running[1], running[2], running[3], losses)
```

```python
import math

import jax
import jax.numpy as jnp
from jax import lax
from jax.sharding import Mesh
from jax.sharding import PartitionSpec as P

D = 2048
HQ = 16
HK = 4
HD = 128
RANK = 64
GROUP = HQ // HK
KVW = HK * HD

EPS = 1e-05
BETA = 0.1
ADAPTER_SCALE = 2.0
THETA = 500000.0

BF = jnp.bfloat16
F32 = jnp.float32

AXES = ("z", "c", "y", "h", "x")
OWN = ("z", "c", "x")


def rotary_tables(positions, half_dim):
    frequency = THETA ** (-(jnp.arange(half_dim, dtype=F32) * 2.0) / (2.0 * half_dim))
    angles = positions.astype(F32)[:, None] * frequency[None, :]
    return (jnp.cos(angles), jnp.sin(angles))


def apply_rotary(values, cosine, sine):
    half = values.shape[-1] // 2
    lower, upper = values[..., :half], values[..., half:]
    return jnp.concatenate([lower * cosine - upper * sine, upper * cosine + lower * sine], axis=-1)


def mm(a, b):
    return jnp.dot(a, b, preferred_element_type=F32)


def attend(queries, keys, values, allowed):
    logits = jnp.einsum("sqkgd,bspkd->skgqbp", queries, keys, preferred_element_type=F32)
    logits = jnp.where(allowed, logits / math.sqrt(HD), -1e30)
    peak = jnp.max(logits, axis=(-2, -1), keepdims=True)
    raised = jnp.exp(logits - peak)
    softmax = raised / jnp.sum(raised, axis=(-2, -1), keepdims=True)
    rounded = softmax.astype(BF)
    mixed = jnp.einsum("skgqbp,bspkd->sqkgd", rounded, values, preferred_element_type=F32)
    return softmax, rounded, mixed


def body(hidden, answer_rows, resp_mask, attn_gain, final_gain, w_query, w_key, w_value, w_out, a_query, b_query, a_value, b_value):
    hidden = hidden[0]
    tokens = hidden.shape[1]
    rows = 2 * tokens
    y_pos, h_pos = lax.axis_index("y"), lax.axis_index("h")

    narrow_v = jnp.concatenate([b_value, jnp.zeros((tokens - b_value.shape[0], RANK), BF)], axis=0)
    packed = jnp.concatenate([w_query, w_key, w_value, w_out, a_query, a_value, b_query, narrow_v], axis=1)
    full = lax.all_gather(packed, OWN, axis=0, tiled=True)
    wq, wk, wv = full[:, :2048], full[:, 2048:2560], full[:, 2560:3072]
    wo = full[:, 3072:5120]
    aq, av = full[:, 5120:5184], full[:, 5184:5248]
    bq = full[:, 5248:5312]
    bv = full[:, 5312:5376].reshape(32, tokens, RANK)[:, : b_value.shape[0]].reshape(KVW, RANK)

    x32 = hidden.astype(F32)
    xn = (x32 * lax.rsqrt(jnp.mean(x32 * x32, axis=-1, keepdims=True) + EPS) * attn_gain).astype(BF)
    other = lax.ppermute(xn, "h", [(0, 1), (1, 0)])
    two = jnp.stack([xn, other])
    every = lax.all_to_all(jnp.broadcast_to(two[None], (4,) + two.shape), "y", 0, 0, tiled=True)
    xa = every.reshape(8 * rows, D)
    xo = xn.reshape(rows, D)

    block = jnp.arange(8, dtype=jnp.int32)
    source = (block // 2) * 2 + jnp.bitwise_xor(block % 2, h_pos)
    key_pos = source[:, None] * tokens + jnp.arange(tokens, dtype=jnp.int32)[None, :]
    own_pos = (y_pos * 2 + h_pos) * tokens + jnp.arange(tokens, dtype=jnp.int32)
    kcos, ksin = rotary_tables(key_pos.reshape(-1), HD // 2)
    kcos = kcos.reshape(8, 1, tokens, 1, HD // 2)
    ksin = ksin.reshape(8, 1, tokens, 1, HD // 2)
    qcos, qsin = rotary_tables(own_pos, HD // 2)
    qcos, qsin = qcos[:, None, None, :], qsin[:, None, None, :]

    kv_shape = (8, 2, tokens, HK, HD)
    keys = apply_rotary(mm(xa, wk).reshape(kv_shape), kcos, ksin).astype(BF)
    v_ref = mm(xa, wv).astype(BF)
    low_v = mm(xa, av).astype(BF)
    v_pol = (lax.optimization_barrier(v_ref).astype(F32) + ADAPTER_SCALE * mm(low_v, bv.T)).astype(BF).reshape(kv_shape)
    v_ref = v_ref.reshape(kv_shape)

    q_shape = (2, tokens, HK, GROUP, HD)
    base_q = mm(xo, wq)
    low_q = mm(xo, aq).astype(BF)
    q_ref = apply_rotary(base_q.reshape(q_shape), qcos, qsin).astype(BF)
    q_pol = apply_rotary((base_q + ADAPTER_SCALE * mm(low_q, bq.T)).reshape(q_shape), qcos, qsin).astype(BF)

    allowed = own_pos[:, None, None] >= key_pos[None]
    _, _, mixed_ref = attend(q_ref, keys, v_ref, allowed)
    soft, prob, mixed_pol = attend(q_pol, keys, v_pol, allowed)

    heads = jnp.concatenate([mixed_ref.astype(BF).reshape(rows, D), mixed_pol.astype(BF).reshape(rows, D)], axis=0)
    proj = mm(heads, wo)
    answers = answer_rows[0].reshape(rows, D).astype(F32)
    response = resp_mask[0].astype(F32)
    x_rows = x32.reshape(rows, D)

    def readout(projected):
        residual = x_rows + projected
        inverse = lax.rsqrt(jnp.mean(residual * residual, axis=-1, keepdims=True) + EPS)
        unit = residual * inverse
        score = jnp.sum(unit * final_gain * answers, axis=-1).reshape(2, tokens)
        return inverse, unit, jnp.sum(response * score, axis=-1)

    _, _, part_ref = readout(proj[:rows])
    inverse, unit, part_pol = readout(proj[rows:])
    difference = part_pol - part_ref
    totals = lax.psum(jnp.broadcast_to((difference[0] - difference[1])[None, None], (8, 128)), "y")
    totals = totals + lax.ppermute(totals, "h", [(0, 1), (1, 0)])
    margin = totals[0, :1]
    loss = jax.nn.softplus(-BETA * margin)
    weight = -BETA * jax.nn.sigmoid(-BETA * margin)

    signed = (response * jnp.array([1.0, -1.0], F32)[:, None]).reshape(rows)
    back_u = (weight * signed)[:, None] * final_gain * answers
    back_y = (inverse * (back_u - unit * jnp.mean(back_u * unit, axis=-1, keepdims=True))).astype(BF)
    back_o = mm(back_y, wo.T).astype(BF).reshape(q_shape)

    row_dot = jnp.transpose(jnp.sum(back_o.astype(F32) * mixed_pol, axis=-1), (0, 2, 3, 1))
    back_prob = jnp.einsum("sqkgd,bspkd->skgqbp", back_o, v_pol, preferred_element_type=F32)
    back_logit = (soft * (back_prob - row_dot[..., None, None]) / math.sqrt(HD)).astype(BF)
    back_q = jnp.einsum("skgqbp,bspkd->sqkgd", back_logit, keys, preferred_element_type=F32)
    back_q = apply_rotary(back_q, qcos, -qsin).astype(BF).reshape(rows, D)
    value_term = jnp.einsum("skgqbp,sqkgd->bspkd", prob, back_o, preferred_element_type=F32).astype(BF).reshape(8 * rows, KVW)

    down_q = mm(back_q, bq).astype(BF)
    down_v = mm(value_term, bv).astype(BF)
    grad_a_q = mm(xo.T, down_q)
    grad_b_q = mm(back_q.T, low_q)
    grad_a_v = mm(xa.T, down_v)
    grad_b_v = mm(value_term.T, low_v).reshape(32, 16, RANK)
    grad_b_v = jnp.concatenate([grad_b_v, jnp.zeros((32, tokens - 16, RANK), F32)], axis=1).reshape(D, RANK)
    grads = ADAPTER_SCALE * jnp.concatenate([grad_a_q, grad_a_v, grad_b_q, grad_b_v], axis=1)
    sent = grads.astype(BF).reshape(32, tokens, 4 * RANK)
    got = lax.all_to_all(sent, OWN, 0, 0, tiled=True)
    mine = jnp.sum(got.astype(F32), axis=0)
    parts = lax.all_to_all(jnp.broadcast_to(mine[None], (8,) + mine.shape), ("y", "h"), 0, 0, tiled=True)
    total = jnp.sum(parts, axis=0)
    return total[:, :64], total[:, 128:192], total[:, 64:128], total[:16, 192:], loss


def solution(mesh):
    fine = Mesh(mesh.devices.reshape(4, 2, 4, 2, 4), AXES)
    seq = ("y", "h")
    weights = P(OWN, None)
    in_specs = (P(OWN, None, seq, None), P(OWN, None, seq, None), P(OWN, None, seq), P(), P()) + (weights,) * 8
    out_specs = (weights,) * 4 + (P(OWN),)
    return jax.shard_map(body, mesh=fine, in_specs=in_specs, out_specs=out_specs, check_vma=False)
```

```python
import math

import jax
import jax.numpy as jnp
from jax import lax
from jax.experimental import pallas as pl
from jax.experimental.pallas import tpu as pltpu
from jax.sharding import Mesh
from jax.sharding import PartitionSpec as P

D = 2048
HQ = 16
HK = 4
HD = 128
RANK = 64
GROUP = HQ // HK
KVW = HK * HD
TOK = 64
ROWS = 2 * TOK
BLOCKS = 8
ALL = BLOCKS * ROWS
L = BLOCKS * TOK
PARTS = 2 * HK
QROWS = GROUP * TOK

EPS = 1e-05
BETA = 0.1
ADAPTER_SCALE = 2.0
THETA = 500000.0

BF = jnp.bfloat16
F32 = jnp.float32

AXES = ("z", "c", "y", "h", "x")
OWN = ("z", "c", "x")


def mm(a, b):
    return jnp.dot(a, b, preferred_element_type=F32)


def mm_t(a, b):
    return lax.dot_general(a, b, (((1,), (1,)), ((), ())), preferred_element_type=F32)


def turn(u, c, s):
    return u * c + pltpu.roll(u, HD // 2, 1) * s


def dot_rows(a, b):
    return jnp.sum(a * b, axis=-1, keepdims=True)


def local_kernel(own_ref, full, xa_in, kc, ks, bias, hid, ans, gain, sign, out,
                 xa, wn, wkv, wq, wo, low, bqm, bvm, keys, vref, vpol, qs, prob, probb, o32, heads, yp, by, bo, bq, vt, dn, sems):
    copies = [
        pltpu.make_async_copy(xa_in, xa, sems.at[0]),
        pltpu.make_async_copy(full.at[:, 5120:5376], wn, sems.at[1]),
        pltpu.make_async_copy(full.at[:, 2048:3072], wkv, sems.at[2]),
        pltpu.make_async_copy(full.at[:, 0:2048], wq, sems.at[3]),
        pltpu.make_async_copy(full.at[:, 3072:5120], wo, sems.at[4]),
    ]
    for copy in copies:
        copy.start()
    own = pl.multiple_of(own_ref[0] * ROWS, ROWS)

    copies[0].wait()
    copies[1].wait()
    lane = lax.broadcasted_iota(jnp.int32, (D, 2 * RANK), 1)
    bqm[...] = jnp.where(lane < RANK, wn[:, 2 * RANK :].astype(F32), 0.0).astype(BF)
    lane16 = lax.broadcasted_iota(jnp.int32, (16, 2 * RANK), 1)
    for d in range(32):
        bvm[16 * d : 16 * d + 16, :] = jnp.where(lane16 >= RANK, wn[64 * d : 64 * d + 16, 2 * RANK :].astype(F32), 0.0).astype(BF)
    copies[2].wait()

    @pl.loop(0, ALL // 256)
    def _(r):
        r0 = pl.multiple_of(r * 256, 256)
        x = xa[pl.ds(r0, 256), :]
        lw = mm(x, wn[:, : 2 * RANK]).astype(BF)
        low[pl.ds(r0, 256), :] = lw
        c, s = kc[pl.ds(r0, 256), :], ks[pl.ds(r0, 256), :]
        kv = mm(x, wkv[...])
        lift = mm_t(lw, bvm[...])
        for g in range(HK):
            cols = slice(HD * g, HD * g + HD)
            k = turn(kv[:, cols], c, s).astype(BF)
            vr = kv[:, KVW + HD * g : KVW + HD * g + HD].astype(BF)
            vp = (vr.astype(F32) + ADAPTER_SCALE * lift[:, cols]).astype(BF)
            for b in range(2):
                t0 = pl.multiple_of(r * 2 * TOK + b * TOK, TOK)
                for side in range(2):
                    src = slice(b * ROWS + side * TOK, b * ROWS + side * TOK + TOK)
                    at = side * HK + g
                    keys[at, pl.ds(t0, TOK), :] = k[src]
                    vref[at, pl.ds(t0, TOK), :] = vr[src]
                    vpol[at, pl.ds(t0, TOK), :] = vp[src]

    copies[3].wait()
    c_own, s_own = kc[pl.ds(own, ROWS), :], ks[pl.ds(own, ROWS), :]

    @pl.loop(0, HK)
    def _(g):
        w0 = pl.multiple_of(g * GROUP * HD, GROUP * HD)
        base = mm(xa[pl.ds(own, ROWS), :], wq[:, pl.ds(w0, GROUP * HD)])
        lift = mm_t(low[pl.ds(own, ROWS), :], bqm[pl.ds(w0, GROUP * HD), :])
        moved = base + ADAPTER_SCALE * lift
        for j in range(GROUP):
            cols = slice(HD * j, HD * j + HD)
            qr = turn(base[:, cols], c_own, s_own).astype(BF)
            qp = turn(moved[:, cols], c_own, s_own).astype(BF)
            for side in range(2):
                src = slice(side * TOK, side * TOK + TOK)
                qs[0, side * HK + g, j * TOK : j * TOK + TOK, :] = qr[src]
                qs[1, side * HK + g, j * TOK : j * TOK + TOK, :] = qp[src]

    scale = 1.0 / math.sqrt(HD)

    def soft(q, k):
        logits = mm_t(q, k) * scale
        logits = (logits.reshape(GROUP, TOK, L) + bias[...][None]).reshape(QROWS, L)
        raised = jnp.exp(logits - jnp.max(logits, axis=-1, keepdims=True))
        return raised * (1.0 / jnp.sum(raised, axis=-1, keepdims=True))

    @pl.loop(0, PARTS)
    def _(i):
        g, side = lax.rem(i, HK), lax.div(i, HK)
        k = keys[i]
        p0 = soft(qs[0, i], k)
        p1 = soft(qs[1, i], k)
        b1 = p1.astype(BF)
        prob[i] = p1
        probb[i] = b1
        m0 = mm(p0.astype(BF), vref[i])
        m1 = mm(b1, vpol[i])
        o32[i] = m1
        n0, n1 = m0.astype(BF), m1.astype(BF)
        r0 = pl.multiple_of(side * TOK, TOK)
        for j in range(GROUP):
            c0 = pl.multiple_of(g * GROUP * HD + j * HD, HD)
            heads[pl.ds(r0, TOK), pl.ds(c0, HD)] = n0[j * TOK : j * TOK + TOK]
            heads[pl.ds(r0 + ROWS, TOK), pl.ds(c0, HD)] = n1[j * TOK : j * TOK + TOK]

    copies[4].wait()
    tile = 512
    zero = jnp.zeros((ROWS, 1), F32)
    sq0, sq1, sc0, sc1 = zero, zero, zero, zero
    for n in range(D // tile):
        cols = slice(n * tile, n * tile + tile)
        y = mm(heads[...], wo[:, cols])
        x = hid[:, cols].astype(F32)
        ga = gain[:, cols] * ans[:, cols].astype(F32)
        y0, y1 = x + y[:ROWS], x + y[ROWS:]
        yp[:, cols] = y1
        sq0, sq1 = sq0 + dot_rows(y0, y0), sq1 + dot_rows(y1, y1)
        sc0, sc1 = sc0 + dot_rows(y0, ga), sc1 + dot_rows(y1, ga)
    inv0 = lax.rsqrt(sq0 * (1.0 / D) + EPS)
    inv1 = lax.rsqrt(sq1 * (1.0 / D) + EPS)
    score0, score1 = sc0 * inv0, sc1 * inv1
    sg = sign[...]
    margin = jnp.sum(sg * (score1 - score0), axis=0, keepdims=True)
    lead = inv1 * sg
    pull = inv1 * score1 * (1.0 / D)
    for n in range(D // tile):
        cols = slice(n * tile, n * tile + tile)
        ga = gain[:, cols] * ans[:, cols].astype(F32)
        by[:, cols] = (lead * (ga - yp[:, cols] * pull)).astype(BF)

    @pl.loop(0, HK)
    def _(g):
        w0 = pl.multiple_of(g * GROUP * HD, GROUP * HD)
        back = mm_t(by[...], wo[pl.ds(w0, GROUP * HD), :]).astype(BF)
        for j in range(GROUP):
            for side in range(2):
                bo[side * HK + g, j * TOK : j * TOK + TOK, :] = back[side * TOK : side * TOK + TOK, HD * j : HD * j + HD]

    @pl.loop(0, PARTS)
    def _(i):
        g, side = lax.rem(i, HK), lax.div(i, HK)
        b = bo[i]
        dp = mm_t(b, vpol[i])
        rd = dot_rows(b.astype(F32), o32[i])
        bl = (prob[i] * (dp - rd) * scale).astype(BF)
        dq = mm(bl, keys[i])
        term = mm(probb[i].T, b).astype(BF)
        r0 = pl.multiple_of(side * TOK, TOK)
        o0 = pl.multiple_of(own + side * TOK, TOK)
        c, s = kc[pl.ds(o0, TOK), :], ks[pl.ds(o0, TOK), :]
        for j in range(GROUP):
            c0 = pl.multiple_of(g * GROUP * HD + j * HD, HD)
            bq[pl.ds(r0, TOK), pl.ds(c0, HD)] = turn(dq[j * TOK : j * TOK + TOK], c, -s).astype(BF)
        for blk in range(BLOCKS):
            v0 = pl.multiple_of(side * TOK + blk * ROWS, TOK)
            vt[pl.ds(v0, TOK), pl.ds(pl.multiple_of(g * HD, HD), HD)] = term[blk * TOK : blk * TOK + TOK]

    dn[...] = mm(vt[...], bvm[...]).astype(BF)
    dq_low = mm(bq[...], bqm[...])
    dn[pl.ds(own, ROWS), :] = (dn[pl.ds(own, ROWS), :].astype(F32) + dq_low).astype(BF)
    dn_t = dn[...].T
    low_t = low[...].T
    low_own_t = low[pl.ds(own, ROWS), :].T
    lane64 = lax.broadcasted_iota(jnp.int32, (256, 2 * RANK), 1)
    for n in range(D // tile):
        cols = slice(n * tile, n * tile + tile)
        ga_t = (ADAPTER_SCALE * mm(dn_t, xa[:, cols])).T
        gb_t = (ADAPTER_SCALE * mm(low_own_t, bq[:, cols])).T
        for d in range(tile // TOK):
            for q in range(4):
                src = slice(d * TOK + q * 16, d * TOK + q * 16 + 16)
                out[q, n * (tile // TOK) + d, :, : 2 * RANK] = ga_t[src].astype(BF)
                out[q, n * (tile // TOK) + d, :, 2 * RANK :] = jnp.where(lane16 < RANK, gb_t[src], 0.0).astype(BF)
    gv_t = (ADAPTER_SCALE * mm(low_t, vt[...])).T
    for d in range(32):
        here = out[0, d, :, 2 * RANK :].astype(F32)
        out[0, d, :, 2 * RANK :] = jnp.where(lane16 < RANK, here, gv_t[16 * d : 16 * d + 16]).astype(BF)
    hi = margin.astype(BF).astype(F32)
    mid = (margin - hi).astype(BF).astype(F32)
    lo = margin - hi - mid
    lane_m = lax.broadcasted_iota(jnp.int32, (16, 4 * RANK), 1)
    riding = jnp.where(lane_m == 0, hi, jnp.where(lane_m == 1, mid, jnp.where(lane_m == 2, lo, 0.0))).astype(BF)
    for q in range(4):
        out[q, 32] = riding


def local_step(own_block, full, xa, kc, ks, bias, hid, ans, gain, sign):
    vm, anyspace = pl.BlockSpec(memory_space=pltpu.VMEM), pl.BlockSpec(memory_space=pl.ANY)
    bf, f32 = (lambda *s: pltpu.VMEM(s, BF)), (lambda *s: pltpu.VMEM(s, F32))
    return pl.pallas_call(
        local_kernel,
        out_shape=jax.ShapeDtypeStruct((4, 33, 16, 4 * RANK), BF),
        in_specs=[pl.BlockSpec(memory_space=pltpu.SMEM), anyspace, anyspace] + [vm] * 7,
        out_specs=vm,
        scratch_shapes=[
            bf(ALL, D), bf(D, 256), bf(D, 2 * KVW), bf(D, D), bf(D, D),
            bf(ALL, 2 * RANK), bf(D, 2 * RANK), bf(KVW, 2 * RANK),
            bf(PARTS, L, HD), bf(PARTS, L, HD), bf(PARTS, L, HD),
            bf(2, PARTS, QROWS, HD), f32(PARTS, QROWS, L), bf(PARTS, QROWS, L), f32(PARTS, QROWS, HD),
            bf(2 * ROWS, D), f32(ROWS, D), bf(ROWS, D), bf(PARTS, QROWS, HD), bf(ROWS, D), bf(ALL, KVW), bf(ALL, 2 * RANK),
            pltpu.SemaphoreType.DMA((5,)),
        ],
        compiler_params=pltpu.CompilerParams(vmem_limit_bytes=60 * 2**20),
        cost_estimate=pl.CostEstimate(flops=24_000_000_000, bytes_accessed=27_000_000, transcendentals=2_100_000),
    )(own_block, full, xa, kc, ks, bias, hid, ans, gain, sign)


def split3(value):
    hi = lax.reduce_precision(value, 8, 7)
    mid = lax.reduce_precision(value - hi, 8, 7)
    return jnp.stack([hi, mid, value - hi - mid], axis=-1)


def body(hidden, answer_rows, resp_mask, attn_gain, final_gain, w_query, w_key, w_value, w_out, a_query, b_query, a_value, b_value):
    hidden = hidden[0]
    y_pos, h_pos = lax.axis_index("y"), lax.axis_index("h")

    narrow_v = jnp.concatenate([b_value, jnp.zeros((TOK - b_value.shape[0], RANK), BF)], axis=0)
    packed = jnp.concatenate([w_query, w_key, w_value, w_out, a_query, a_value, b_query, narrow_v], axis=1)
    full = lax.all_gather(packed, OWN, axis=0, tiled=True)

    x32 = hidden.astype(F32)
    xn = (x32 * lax.rsqrt(jnp.mean(x32 * x32, axis=-1, keepdims=True) + EPS) * attn_gain).astype(BF).reshape(ROWS, D)
    other = lax.ppermute(xn, "h", [(0, 1), (1, 0)])
    two = jnp.concatenate([xn, other], axis=0)
    every = lax.all_to_all(jnp.broadcast_to(two[None], (4,) + two.shape), "y", 0, 0, tiled=True)
    xa = every.reshape(ALL, D)

    block = jnp.arange(BLOCKS, dtype=jnp.int32)
    source = (block // 2) * 2 + jnp.bitwise_xor(block % 2, h_pos)
    token = jnp.arange(TOK, dtype=jnp.int32)
    key_pos = source[:, None] * TOK + token[None, :]
    own_pos = (y_pos * 2 + h_pos) * TOK + token
    frequency = THETA ** (-(jnp.arange(HD // 2, dtype=F32) * 2.0) / HD)
    row_pos = jnp.broadcast_to(key_pos[:, None, :], (BLOCKS, 2, TOK)).reshape(ALL)
    angles = row_pos.astype(F32)[:, None] * frequency[None, :]
    cosine, sine = jnp.cos(angles), jnp.sin(angles)
    kc = jnp.concatenate([cosine, cosine], axis=1)
    ks = jnp.concatenate([-sine, sine], axis=1)
    bias = jnp.where(own_pos[:, None] >= key_pos.reshape(1, L), 0.0, -1e30).astype(F32)
    sign = (resp_mask[0].astype(F32) * jnp.array([1.0, -1.0], F32)[:, None]).reshape(ROWS, 1)
    own_block = jnp.full((1,), 2, jnp.int32) * y_pos

    mine = local_step(own_block, full, xa, kc, ks, bias, hidden.reshape(ROWS, D), answer_rows.reshape(ROWS, D), final_gain.reshape(1, D), sign)

    got = jnp.sum(lax.all_to_all(mine, "y", 0, 0, tiled=True).astype(F32), axis=0)
    first = jnp.sum(got[32, 0, :3]).reshape(1)
    sent = got.astype(BF)
    sent = jnp.concatenate([sent[:32], jnp.pad(split3(first).astype(BF).reshape(1, 1, 3), ((0, 0), (0, 15), (0, 253)))], axis=0)
    sent = lax.optimization_barrier(sent)
    met = lax.ppermute(sent, "h", [(0, 1), (1, 0)])
    margin = jnp.sum(sent[32, 0, :3].astype(F32)).reshape(1) + jnp.sum(met[32, 0, :3].astype(F32)).reshape(1)
    loss = jax.nn.softplus(-BETA * margin)
    weight = -BETA * jax.nn.sigmoid(-BETA * margin)
    scaled = (weight * (sent[:32].astype(F32) + met[:32].astype(F32))).astype(BF)
    shares = lax.all_to_all(scaled, OWN, 0, 0, tiled=True)
    piece = jnp.sum(shares.astype(F32), axis=0)
    total = lax.all_to_all(jnp.broadcast_to(piece[None], (4,) + piece.shape), "y", 0, 0, tiled=True).reshape(TOK, 4 * RANK)
    return total[:, :64], total[:, 128:192], total[:, 64:128], total[:16, 192:], loss


def solution(mesh):
    fine = Mesh(mesh.devices.reshape(4, 2, 4, 2, 4), AXES)
    seq = ("y", "h")
    weights = P(OWN, None)
    in_specs = (P(OWN, None, seq, None), P(OWN, None, seq, None), P(OWN, None, seq), P(), P()) + (weights,) * 8
    out_specs = (weights,) * 4 + (P(OWN),)
    return jax.shard_map(body, mesh=fine, in_specs=in_specs, out_specs=out_specs, check_vma=False)
```

```python
import math

import jax
import jax.numpy as jnp
from jax import lax
from jax.experimental import pallas as pl
from jax.experimental.pallas import tpu as pltpu
from jax.sharding import Mesh
from jax.sharding import PartitionSpec as P

D = 2048
HQ = 16
HK = 4
HD = 128
RANK = 64
GROUP = HQ // HK
KVW = HK * HD
TOK = 64
ROWS = 2 * TOK
BLOCKS = 8
ALL = BLOCKS * ROWS
L = BLOCKS * TOK
PARTS = 2 * HK
QROWS = GROUP * TOK

EPS = 1e-05
BETA = 0.1
ADAPTER_SCALE = 2.0
THETA = 500000.0

BF = jnp.bfloat16
F32 = jnp.float32

AXES = ("z", "c", "y", "h", "x")
OWN = ("z", "c", "x")


def mm(a, b):
    return jnp.dot(a, b, preferred_element_type=F32)


def mm_t(a, b):
    return lax.dot_general(a, b, (((1,), (1,)), ((), ())), preferred_element_type=F32)


def turn(u, c, s):
    return u * c + pltpu.roll(u, HD // 2, 1) * s


def dot_rows(a, b):
    return jnp.sum(a * b, axis=-1, keepdims=True)


def local_kernel(own_ref, full, xa, kc, ks, bias, hid, ans, gain, sign, out,
                 wn, wkv, wq, wo, low, bqm, bvm, keys, vref, vpol, qs, prob, probb, o32, heads, yp, by, bo, bq, vt, dn, sems):
    copies = [
        pltpu.make_async_copy(full.at[0, :, 0:256], wn, sems.at[0]),
        pltpu.make_async_copy(full.at[1, :, 0:1024], wkv, sems.at[1]),
        pltpu.make_async_copy(full.at[0, :, 256:2304], wq, sems.at[2]),
        pltpu.make_async_copy(full.at[0, :, 2304:2688], wo.at[:, 0:384], sems.at[3]),
        pltpu.make_async_copy(full.at[1, :, 1024:2688], wo.at[:, 384:2048], sems.at[4]),
    ]
    for copy in copies:
        copy.start()
    own = pl.multiple_of(own_ref[0] * ROWS, ROWS)

    copies[0].wait()
    lane = lax.broadcasted_iota(jnp.int32, (D, 2 * RANK), 1)
    bqm[...] = jnp.where(lane < RANK, wn[:, 2 * RANK :].astype(F32), 0.0).astype(BF)
    lane16 = lax.broadcasted_iota(jnp.int32, (16, 2 * RANK), 1)
    for d in range(32):
        bvm[16 * d : 16 * d + 16, :] = jnp.where(lane16 >= RANK, wn[64 * d : 64 * d + 16, 2 * RANK :].astype(F32), 0.0).astype(BF)
    copies[1].wait()

    @pl.loop(0, ALL // 256)
    def _(r):
        r0 = pl.multiple_of(r * 256, 256)
        x = xa[pl.ds(r0, 256), :]
        lw = mm(x, wn[:, : 2 * RANK]).astype(BF)
        low[pl.ds(r0, 256), :] = lw
        c, s = kc[pl.ds(r0, 256), :], ks[pl.ds(r0, 256), :]
        kv = mm(x, wkv[...])
        lift = mm_t(lw, bvm[...])
        for g in range(HK):
            cols = slice(HD * g, HD * g + HD)
            k = turn(kv[:, cols], c, s).astype(BF)
            vr = kv[:, KVW + HD * g : KVW + HD * g + HD].astype(BF)
            vp = (vr.astype(F32) + ADAPTER_SCALE * lift[:, cols]).astype(BF)
            for b in range(2):
                t0 = pl.multiple_of(r * 2 * TOK + b * TOK, TOK)
                for side in range(2):
                    src = slice(b * ROWS + side * TOK, b * ROWS + side * TOK + TOK)
                    at = side * HK + g
                    keys[at, pl.ds(t0, TOK), :] = k[src]
                    vref[at, pl.ds(t0, TOK), :] = vr[src]
                    vpol[at, pl.ds(t0, TOK), :] = vp[src]

    copies[2].wait()
    c_own, s_own = kc[pl.ds(own, ROWS), :], ks[pl.ds(own, ROWS), :]

    @pl.loop(0, HK)
    def _(g):
        w0 = pl.multiple_of(g * GROUP * HD, GROUP * HD)
        base = mm(xa[pl.ds(own, ROWS), :], wq[:, pl.ds(w0, GROUP * HD)])
        lift = mm_t(low[pl.ds(own, ROWS), :], bqm[pl.ds(w0, GROUP * HD), :])
        moved = base + ADAPTER_SCALE * lift
        for j in range(GROUP):
            cols = slice(HD * j, HD * j + HD)
            qr = turn(base[:, cols], c_own, s_own).astype(BF)
            qp = turn(moved[:, cols], c_own, s_own).astype(BF)
            for side in range(2):
                src = slice(side * TOK, side * TOK + TOK)
                qs[0, side * HK + g, j * TOK : j * TOK + TOK, :] = qr[src]
                qs[1, side * HK + g, j * TOK : j * TOK + TOK, :] = qp[src]

    scale = 1.0 / math.sqrt(HD)

    def soft(q, k):
        logits = mm_t(q, k) * scale
        logits = (logits.reshape(GROUP, TOK, L) + bias[...][None]).reshape(QROWS, L)
        raised = jnp.exp(logits - jnp.max(logits, axis=-1, keepdims=True))
        return raised * (1.0 / jnp.sum(raised, axis=-1, keepdims=True))

    @pl.loop(0, PARTS)
    def _(i):
        g, side = lax.rem(i, HK), lax.div(i, HK)
        k = keys[i]
        p0 = soft(qs[0, i], k)
        p1 = soft(qs[1, i], k)
        b1 = p1.astype(BF)
        prob[i] = p1
        probb[i] = b1
        m0 = mm(p0.astype(BF), vref[i])
        m1 = mm(b1, vpol[i])
        o32[i] = m1
        n0, n1 = m0.astype(BF), m1.astype(BF)
        r0 = pl.multiple_of(side * TOK, TOK)
        for j in range(GROUP):
            c0 = pl.multiple_of(g * GROUP * HD + j * HD, HD)
            heads[pl.ds(r0, TOK), pl.ds(c0, HD)] = n0[j * TOK : j * TOK + TOK]
            heads[pl.ds(r0 + ROWS, TOK), pl.ds(c0, HD)] = n1[j * TOK : j * TOK + TOK]

    copies[3].wait()
    copies[4].wait()
    tile = 512
    zero = jnp.zeros((ROWS, 1), F32)
    sq0, sq1, sc0, sc1 = zero, zero, zero, zero
    for n in range(D // tile):
        cols = slice(n * tile, n * tile + tile)
        y = mm(heads[...], wo[:, cols])
        x = hid[:, cols].astype(F32)
        ga = gain[:, cols] * ans[:, cols].astype(F32)
        y0, y1 = x + y[:ROWS], x + y[ROWS:]
        yp[:, cols] = y1
        sq0, sq1 = sq0 + dot_rows(y0, y0), sq1 + dot_rows(y1, y1)
        sc0, sc1 = sc0 + dot_rows(y0, ga), sc1 + dot_rows(y1, ga)
    inv0 = lax.rsqrt(sq0 * (1.0 / D) + EPS)
    inv1 = lax.rsqrt(sq1 * (1.0 / D) + EPS)
    score0, score1 = sc0 * inv0, sc1 * inv1
    sg = sign[...]
    margin = jnp.sum(sg * (score1 - score0), axis=0, keepdims=True)
    lead = inv1 * sg
    pull = inv1 * score1 * (1.0 / D)
    for n in range(D // tile):
        cols = slice(n * tile, n * tile + tile)
        ga = gain[:, cols] * ans[:, cols].astype(F32)
        by[:, cols] = (lead * (ga - yp[:, cols] * pull)).astype(BF)

    @pl.loop(0, HK)
    def _(g):
        w0 = pl.multiple_of(g * GROUP * HD, GROUP * HD)
        back = mm_t(by[...], wo[pl.ds(w0, GROUP * HD), :]).astype(BF)
        for j in range(GROUP):
            for side in range(2):
                bo[side * HK + g, j * TOK : j * TOK + TOK, :] = back[side * TOK : side * TOK + TOK, HD * j : HD * j + HD]

    @pl.loop(0, PARTS)
    def _(i):
        g, side = lax.rem(i, HK), lax.div(i, HK)
        b = bo[i]
        dp = mm_t(b, vpol[i])
        rd = dot_rows(b.astype(F32), o32[i])
        bl = (prob[i] * (dp - rd) * scale).astype(BF)
        dq = mm(bl, keys[i])
        term = mm(probb[i].T, b).astype(BF)
        r0 = pl.multiple_of(side * TOK, TOK)
        o0 = pl.multiple_of(own + side * TOK, TOK)
        c, s = kc[pl.ds(o0, TOK), :], ks[pl.ds(o0, TOK), :]
        for j in range(GROUP):
            c0 = pl.multiple_of(g * GROUP * HD + j * HD, HD)
            bq[pl.ds(r0, TOK), pl.ds(c0, HD)] = turn(dq[j * TOK : j * TOK + TOK], c, -s).astype(BF)
        for blk in range(BLOCKS):
            v0 = pl.multiple_of(side * TOK + blk * ROWS, TOK)
            vt[pl.ds(v0, TOK), pl.ds(pl.multiple_of(g * HD, HD), HD)] = term[blk * TOK : blk * TOK + TOK]

    dn[...] = mm(vt[...], bvm[...]).astype(BF)
    dq_low = mm(bq[...], bqm[...])
    dn[pl.ds(own, ROWS), :] = (dn[pl.ds(own, ROWS), :].astype(F32) + dq_low).astype(BF)
    dn_t = dn[...].T
    low_t = low[...].T
    low_own_t = low[pl.ds(own, ROWS), :].T
    left = lane16 < RANK
    for n in range(D // tile):
        cols = slice(n * tile, n * tile + tile)
        ga_t = (ADAPTER_SCALE * mm(dn_t, xa[:, cols])).T
        gb_t = (ADAPTER_SCALE * mm(low_own_t, bq[:, cols])).T
        for d in range(tile // TOK):
            at = n * (tile // TOK) + d
            ga, gb = ga_t[d * TOK : d * TOK + TOK], gb_t[d * TOK : d * TOK + TOK]
            for q in range(4):
                out[q, at] = ga[q * 16 : q * 16 + 16].astype(BF)
            for q in range(2):
                out[4 + q, at] = jnp.where(left, gb[q * 32 : q * 32 + 16], pltpu.roll(gb[q * 32 + 16 : q * 32 + 32], RANK, 1)).astype(BF)
    gv_t = (ADAPTER_SCALE * mm(low_t, vt[...])).T
    for d in range(32):
        out[6, d] = jnp.where(left, pltpu.roll(gv_t[16 * d : 16 * d + 16], RANK, 1), 0.0).astype(BF)
        out[7, d] = jnp.zeros((16, 2 * RANK), BF)
    hi = margin.astype(BF).astype(F32)
    mid = (margin - hi).astype(BF).astype(F32)
    lo = margin - hi - mid
    riding = jnp.where(lane16 == 0, hi, jnp.where(lane16 == 1, mid, jnp.where(lane16 == 2, lo, 0.0))).astype(BF)
    for q in range(8):
        out[q, 32] = riding


def scale_kernel(got, scaled, margin_out):
    ride = got[0, 32].astype(F32)
    for q in range(1, 8):
        ride = ride + got[q, 32].astype(F32)
    margin = jnp.sum(ride[0:1, :], axis=-1, keepdims=True)
    margin_out[...] = jnp.broadcast_to(margin, (8, 2 * RANK))
    weight = -BETA / (1.0 + jnp.exp(BETA * margin))
    total = got[0, 0:32].astype(F32)
    for q in range(1, 8):
        total = total + got[q, 0:32].astype(F32)
    scaled[...] = (total * weight[None]).astype(BF)


def scale_step(got):
    vm = pl.BlockSpec(memory_space=pltpu.VMEM)
    return pl.pallas_call(
        scale_kernel,
        out_shape=(jax.ShapeDtypeStruct((32, 16, 2 * RANK), BF), jax.ShapeDtypeStruct((8, 2 * RANK), F32)),
        in_specs=[vm],
        out_specs=(vm, vm),
        compiler_params=pltpu.CompilerParams(vmem_limit_bytes=16 * 2**20),
    )(got)


def local_step(own_block, full, xa, kc, ks, bias, hid, ans, gain, sign):
    vm, anyspace = pl.BlockSpec(memory_space=pltpu.VMEM), pl.BlockSpec(memory_space=pl.ANY)
    bf, f32 = (lambda *s: pltpu.VMEM(s, BF)), (lambda *s: pltpu.VMEM(s, F32))
    return pl.pallas_call(
        local_kernel,
        out_shape=jax.ShapeDtypeStruct((8, 33, 16, 2 * RANK), BF),
        in_specs=[pl.BlockSpec(memory_space=pltpu.SMEM), anyspace] + [vm] * 8,
        out_specs=vm,
        scratch_shapes=[
            bf(D, 256), bf(D, 2 * KVW), bf(D, D), bf(D, D),
            bf(ALL, 2 * RANK), bf(D, 2 * RANK), bf(KVW, 2 * RANK),
            bf(PARTS, L, HD), bf(PARTS, L, HD), bf(PARTS, L, HD),
            bf(2, PARTS, QROWS, HD), f32(PARTS, QROWS, L), bf(PARTS, QROWS, L), f32(PARTS, QROWS, HD),
            bf(2 * ROWS, D), f32(ROWS, D), bf(ROWS, D), bf(PARTS, QROWS, HD), bf(ROWS, D), bf(ALL, KVW), bf(ALL, 2 * RANK),
            pltpu.SemaphoreType.DMA((5,)),
        ],
        compiler_params=pltpu.CompilerParams(vmem_limit_bytes=50 * 2**20),
        cost_estimate=pl.CostEstimate(flops=24_000_000_000, bytes_accessed=27_000_000, transcendentals=2_100_000),
    )(own_block, full, xa, kc, ks, bias, hid, ans, gain, sign)


def body(hidden, answer_rows, resp_mask, attn_gain, final_gain, w_query, w_key, w_value, w_out, a_query, b_query, a_value, b_value):
    hidden = hidden[0]
    y_pos, h_pos = lax.axis_index("y"), lax.axis_index("h")

    narrow_v = jnp.concatenate([b_value, jnp.zeros((TOK - b_value.shape[0], RANK), BF)], axis=0)
    half0 = jnp.concatenate([a_query, a_value, b_query, narrow_v, w_query, w_out[:, :384]], axis=1)
    half1 = jnp.concatenate([w_key, w_value, w_out[:, 384:]], axis=1)
    packed = jnp.where(h_pos == 0, half0, half1)
    full = lax.all_gather(packed, ("h",) + OWN, axis=0, tiled=True).reshape(2, D, half0.shape[1])

    x32 = hidden.astype(F32)
    xn = (x32 * lax.rsqrt(jnp.mean(x32 * x32, axis=-1, keepdims=True) + EPS) * attn_gain).astype(BF).reshape(ROWS, D)
    other = lax.ppermute(xn, "h", [(0, 1), (1, 0)])
    two = jnp.concatenate([xn, other], axis=0)
    every = lax.all_to_all(jnp.broadcast_to(two[None], (4,) + two.shape), "y", 0, 0, tiled=True)
    xa = every.reshape(ALL, D)

    block = jnp.arange(BLOCKS, dtype=jnp.int32)
    source = (block // 2) * 2 + jnp.bitwise_xor(block % 2, h_pos)
    token = jnp.arange(TOK, dtype=jnp.int32)
    key_pos = source[:, None] * TOK + token[None, :]
    own_pos = (y_pos * 2 + h_pos) * TOK + token
    frequency = THETA ** (-(jnp.arange(HD // 2, dtype=F32) * 2.0) / HD)
    row_pos = jnp.broadcast_to(key_pos[:, None, :], (BLOCKS, 2, TOK)).reshape(ALL)
    angles = row_pos.astype(F32)[:, None] * frequency[None, :]
    cosine, sine = jnp.cos(angles), jnp.sin(angles)
    kc = jnp.concatenate([cosine, cosine], axis=1)
    ks = jnp.concatenate([-sine, sine], axis=1)
    bias = jnp.where(own_pos[:, None] >= key_pos.reshape(1, L), 0.0, -1e30).astype(F32)
    sign = (resp_mask[0].astype(F32) * jnp.array([1.0, -1.0], F32)[:, None]).reshape(ROWS, 1)
    own_block = jnp.full((1,), 2, jnp.int32) * y_pos

    mine = local_step(own_block, full, xa, kc, ks, bias, hidden.reshape(ROWS, D), answer_rows.reshape(ROWS, D), final_gain.reshape(1, D), sign)

    seq = ("y", "h")
    scaled, margin = scale_step(lax.all_to_all(mine, seq, 0, 0, tiled=True))
    shares = lax.all_to_all(scaled, OWN, 0, 0, tiled=True)
    loss = jax.nn.softplus(-BETA * margin[0, :1])
    piece = jnp.sum(shares.astype(F32), axis=0)
    total = lax.all_to_all(jnp.broadcast_to(piece[None], (8,) + piece.shape), seq, 0, 0, tiled=True)
    grad_a = total[:4].reshape(TOK, 2 * RANK)
    low_half, high_half = total[4:6, :, :RANK], total[4:6, :, RANK:]
    grad_b_q = jnp.stack([low_half, high_half], axis=1).reshape(TOK, RANK)
    return grad_a[:, :RANK], grad_b_q, grad_a[:, RANK:], total[6, :, :RANK], loss


def solution(mesh):
    fine = Mesh(mesh.devices.reshape(4, 2, 4, 2, 4), AXES)
    seq = ("y", "h")
    weights = P(OWN, None)
    in_specs = (P(OWN, None, seq, None), P(OWN, None, seq, None), P(OWN, None, seq), P(), P()) + (weights,) * 8
    out_specs = (weights,) * 4 + (P(OWN),)
    return jax.shard_map(body, mesh=fine, in_specs=in_specs, out_specs=out_specs, check_vma=False)
```

```python
import math

import jax
import jax.numpy as jnp
from jax import lax
from jax.experimental import pallas as pl
from jax.experimental.pallas import tpu as pltpu
from jax.sharding import Mesh
from jax.sharding import PartitionSpec as P

D = 2048
HQ = 16
HK = 4
HD = 128
RANK = 64
GROUP = HQ // HK
KVW = HK * HD
TOK = 64
ROWS = 2 * TOK
BLOCKS = 8
ALL = BLOCKS * ROWS
L = BLOCKS * TOK
PARTS = 2 * HK
QROWS = GROUP * TOK
PIECES = 4

EPS = 1e-05
BETA = 0.1
ADAPTER_SCALE = 2.0
THETA = 500000.0

BF = jnp.bfloat16
F32 = jnp.float32

AXES = ("z", "c", "y", "h", "x")
OWN = ("z", "c", "x")


def mm(a, b):
    return jnp.dot(a, b, preferred_element_type=F32)


def mm_t(a, b):
    return lax.dot_general(a, b, (((1,), (1,)), ((), ())), preferred_element_type=F32)


def turn(u, c, s):
    return u * c + pltpu.roll(u, HD // 2, 1) * s


def dot_rows(a, b):
    return jnp.sum(a * b, axis=-1, keepdims=True)


def split3(margin):
    lane = lax.broadcasted_iota(jnp.int32, (16, 2 * RANK), 1)
    hi = margin.astype(BF).astype(F32)
    mid = (margin - hi).astype(BF).astype(F32)
    lo = margin - hi - mid
    return jnp.where(lane == 0, hi, jnp.where(lane == 1, mid, jnp.where(lane == 2, lo, 0.0))).astype(BF)


def local_kernel(own_ref, full, xa, kc, ks, bias, hid, ans, gain, sign, out,
                 wn, wkv, wq, wo, low, bv, keys, vref, vpol, qs, prob, probb, o32, heads, yp, by, bo, bq, vt, dn, sems):
    half = D // PIECES

    def pieces(first, h, cols, dst, at):
        made = []
        for n in range(PIECES):
            rows = pl.ds(n * half, half)
            made.append(pltpu.make_async_copy(full.at[h, rows, cols[0] : cols[1]], dst.at[rows, at[0] : at[1]], sems.at[first, n]))
        return made

    copies = [
        pieces(0, 0, (0, 256), wn, (0, 256)),
        pieces(1, 1, (0, 1024), wkv, (0, 1024)),
        pieces(2, 0, (256, 2304), wq, (0, 2048)),
        pieces(3, 0, (2304, 2688), wo, (0, 384)),
        pieces(4, 1, (1024, 2688), wo, (384, 2048)),
    ]
    def begin(first):
        for copy in copies[first]:
            copy.start()

    def arrived(first):
        for copy in copies[first]:
            copy.wait()

    begin(0)
    begin(1)

    own = pl.multiple_of(own_ref[0] * ROWS, ROWS)

    arrived(0)
    lane_of = lambda n: lax.broadcasted_iota(jnp.int32, (n, 2 * RANK), 1)
    for d in range(32):
        bv[16 * d : 16 * d + 16, :] = wn[64 * d : 64 * d + 16, 2 * RANK :]
    arrived(1)
    begin(2)

    @pl.loop(0, ALL // 256, unroll=2)
    def _(r):
        r0 = pl.multiple_of(r * 256, 256)
        x = xa[pl.ds(r0, 256), :]
        lw = mm(x, wn[:, : 2 * RANK])
        low[pl.ds(r0, 256), :] = lw.astype(BF)
        c, s = kc[pl.ds(r0, 256), :], ks[pl.ds(r0, 256), :]
        kv = mm(x, wkv[...])
        lift = mm_t(jnp.where(lane_of(256) < RANK, 0.0, lw).astype(BF), bv[...])
        for g in range(HK):
            cols = slice(HD * g, HD * g + HD)
            k = turn(kv[:, cols], c, s).astype(BF)
            vr = kv[:, KVW + HD * g : KVW + HD * g + HD].astype(BF)
            vp = (vr.astype(F32) + ADAPTER_SCALE * lift[:, cols]).astype(BF)
            for b in range(2):
                t0 = pl.multiple_of(r * 2 * TOK + b * TOK, TOK)
                for side in range(2):
                    src = slice(b * ROWS + side * TOK, b * ROWS + side * TOK + TOK)
                    at = side * HK + g
                    keys[at, pl.ds(t0, TOK), :] = k[src]
                    vref[at, pl.ds(t0, TOK), :] = vr[src]
                    vpol[at, pl.ds(t0, TOK), :] = vp[src]

    arrived(2)
    begin(3)
    begin(4)
    low_own = low[pl.ds(own, ROWS), :].astype(F32)
    low_q = jnp.where(lane_of(ROWS) < RANK, low_own, 0.0).astype(BF)
    c_own, s_own = kc[pl.ds(own, ROWS), :], ks[pl.ds(own, ROWS), :]

    @pl.loop(0, HK, unroll=True)
    def _(g):
        w0 = pl.multiple_of(g * GROUP * HD, GROUP * HD)
        base = mm(xa[pl.ds(own, ROWS), :], wq[:, pl.ds(w0, GROUP * HD)])
        lift = mm_t(low_q, wn[pl.ds(w0, GROUP * HD), 2 * RANK :])
        moved = base + ADAPTER_SCALE * lift
        for j in range(GROUP):
            cols = slice(HD * j, HD * j + HD)
            qr = turn(base[:, cols], c_own, s_own).astype(BF)
            qp = turn(moved[:, cols], c_own, s_own).astype(BF)
            for side in range(2):
                src = slice(side * TOK, side * TOK + TOK)
                qs[0, side * HK + g, j * TOK : j * TOK + TOK, :] = qr[src]
                qs[1, side * HK + g, j * TOK : j * TOK + TOK, :] = qp[src]

    scale = 1.0 / math.sqrt(HD)

    def soft(q, k):
        logits = mm_t(q, k).reshape(GROUP, TOK, L) * (scale * math.log2(math.e)) + bias[...][None]
        logits = logits.reshape(QROWS, L)
        raised = jnp.exp2(logits - jnp.max(logits, axis=-1, keepdims=True))
        return raised * (1.0 / jnp.sum(raised, axis=-1, keepdims=True))

    @pl.loop(0, PARTS, unroll=2)
    def _(i):
        g, side = lax.rem(i, HK), lax.div(i, HK)
        k = keys[i]
        p0 = soft(qs[0, i], k)
        p1 = soft(qs[1, i], k)
        b1 = p1.astype(BF)
        prob[i] = p1
        probb[i] = b1
        m0 = mm(p0.astype(BF), vref[i])
        m1 = mm(b1, vpol[i])
        o32[i] = m1
        n0, n1 = m0.astype(BF), m1.astype(BF)
        r0 = pl.multiple_of(side * TOK, TOK)
        for j in range(GROUP):
            c0 = pl.multiple_of(g * GROUP * HD + j * HD, HD)
            heads[pl.ds(r0, TOK), pl.ds(c0, HD)] = n0[j * TOK : j * TOK + TOK]
            heads[pl.ds(r0 + ROWS, TOK), pl.ds(c0, HD)] = n1[j * TOK : j * TOK + TOK]

    arrived(3)
    arrived(4)
    tile = 512
    zero = jnp.zeros((ROWS, 1), F32)
    sq0, sq1, sc0, sc1 = zero, zero, zero, zero
    for n in range(D // tile):
        cols = slice(n * tile, n * tile + tile)
        y = mm(heads[...], wo[:, cols])
        x = hid[:, cols].astype(F32)
        ga = gain[:, cols] * ans[:, cols].astype(F32)
        y0, y1 = x + y[:ROWS], x + y[ROWS:]
        yp[:, cols] = y1
        sq0, sq1 = sq0 + dot_rows(y0, y0), sq1 + dot_rows(y1, y1)
        sc0, sc1 = sc0 + dot_rows(y0, ga), sc1 + dot_rows(y1, ga)
    inv0 = lax.rsqrt(sq0 * (1.0 / D) + EPS)
    inv1 = lax.rsqrt(sq1 * (1.0 / D) + EPS)
    score0, score1 = sc0 * inv0, sc1 * inv1
    sg = sign[...]
    margin = jnp.sum(sg * (score1 - score0), axis=0, keepdims=True)
    lead = inv1 * sg
    pull = inv1 * score1 * (1.0 / D)
    for n in range(D // tile):
        cols = slice(n * tile, n * tile + tile)
        ga = gain[:, cols] * ans[:, cols].astype(F32)
        by[:, cols] = (lead * (ga - yp[:, cols] * pull)).astype(BF)

    by_t = by[...].T

    @pl.loop(0, HK, unroll=True)
    def _(g):
        w0 = pl.multiple_of(g * GROUP * HD, GROUP * HD)
        back = mm(wo[pl.ds(w0, GROUP * HD), :], by_t).T.astype(BF)
        for j in range(GROUP):
            for side in range(2):
                bo[side * HK + g, j * TOK : j * TOK + TOK, :] = back[side * TOK : side * TOK + TOK, HD * j : HD * j + HD]

    @pl.loop(0, PARTS, unroll=2)
    def _(i):
        g, side = lax.rem(i, HK), lax.div(i, HK)
        b = bo[i]
        dp = mm_t(b, vpol[i])
        rd = dot_rows(b.astype(F32), o32[i]) * scale
        bl = (prob[i] * (dp * scale - rd)).astype(BF)
        dq = mm(bl, keys[i])
        term = mm(probb[i].T, b).astype(BF)
        r0 = pl.multiple_of(side * TOK, TOK)
        o0 = pl.multiple_of(own + side * TOK, TOK)
        c, s = kc[pl.ds(o0, TOK), :], ks[pl.ds(o0, TOK), :]
        for j in range(GROUP):
            c0 = pl.multiple_of(g * GROUP * HD + j * HD, HD)
            bq[pl.ds(r0, TOK), pl.ds(c0, HD)] = turn(dq[j * TOK : j * TOK + TOK], c, -s).astype(BF)
        for blk in range(BLOCKS):
            v0 = pl.multiple_of(side * TOK + blk * ROWS, TOK)
            vt[pl.ds(v0, TOK), pl.ds(pl.multiple_of(g * HD, HD), HD)] = term[blk * TOK : blk * TOK + TOK]

    dn[...] = jnp.where(lane_of(ALL) < RANK, 0.0, mm(vt[...], bv[...])).astype(BF)
    dq_low = jnp.where(lane_of(ROWS) < RANK, mm(bq[...], wn[:, 2 * RANK :]), 0.0)
    dn[pl.ds(own, ROWS), :] = (dn[pl.ds(own, ROWS), :].astype(F32) + dq_low).astype(BF)
    dn_t = dn[...].T
    low_t = low[...].T
    low_own_t = low[pl.ds(own, ROWS), :].T
    lane16 = lane_of(16)
    left = lane16 < RANK
    for n in range(D // tile):
        cols = slice(n * tile, n * tile + tile)
        ga_t = (ADAPTER_SCALE * mm(dn_t, xa[:, cols])).T
        gb_t = (ADAPTER_SCALE * mm(low_own_t, bq[:, cols])).T
        for d in range(tile // TOK):
            at = n * (tile // TOK) + d
            ga, gb = ga_t[d * TOK : d * TOK + TOK], gb_t[d * TOK : d * TOK + TOK]
            for q in range(4):
                out[q, at] = ga[q * 16 : q * 16 + 16].astype(BF)
            for q in range(2):
                out[4 + q, at] = jnp.where(left, gb[q * 32 : q * 32 + 16], pltpu.roll(gb[q * 32 + 16 : q * 32 + 32], RANK, 1)).astype(BF)
    gv_t = (ADAPTER_SCALE * mm(low_t, vt[...])).T
    for d in range(32):
        out[6, d] = jnp.where(left, pltpu.roll(gv_t[16 * d : 16 * d + 16], RANK, 1), 0.0).astype(BF)
        out[7, d] = jnp.zeros((16, 2 * RANK), BF)
    riding = split3(margin)
    for q in range(8):
        out[q, 32] = riding


def ride_of(block):
    return jnp.sum(block[0:1, :], axis=-1, keepdims=True)


def halves_kernel(h_ref, got, keep, send, margin_out):
    h = h_ref[0]
    ride = got[0, 0, 32].astype(F32)
    kept, sent = got[0, h, 0:32].astype(F32), got[0, 1 - h, 0:32].astype(F32)
    for q in range(1, 4):
        ride = ride + got[q, 0, 32].astype(F32)
        kept = kept + got[q, h, 0:32].astype(F32)
        sent = sent + got[q, 1 - h, 0:32].astype(F32)
    margin = ride_of(ride)
    margin_out[...] = jnp.broadcast_to(margin, (8, 2 * RANK))
    keep[...] = kept
    send[0:32] = sent.astype(BF)
    send[32] = split3(margin)


def scale_kernel(keep, met, margin_in, scaled, margin_out):
    margin = margin_in[0:1, 0:1] + ride_of(met[32].astype(F32))
    margin_out[...] = jnp.broadcast_to(margin, (8, 2 * RANK))
    weight = -BETA / (1.0 + jnp.exp(BETA * margin))
    scaled[...] = ((keep[...] + met[0:32].astype(F32)) * weight[None]).astype(BF)


def small_call(kernel, out_shape, args, scalars):
    vm = pl.BlockSpec(memory_space=pltpu.VMEM)
    return pl.pallas_call(
        kernel,
        out_shape=out_shape,
        in_specs=[pl.BlockSpec(memory_space=pltpu.SMEM)] * scalars + [vm] * (len(args) - scalars),
        out_specs=(vm,) * len(out_shape),
        compiler_params=pltpu.CompilerParams(vmem_limit_bytes=16 * 2**20),
    )(*args)


def pack_kernel(h_ref, wq, wk, wv, wo, aq, av, bq, bv, out, narrow, sems):
    narrow[:, 0:RANK] = aq[...]
    narrow[:, RANK : 2 * RANK] = av[...]
    narrow[:, 2 * RANK : 3 * RANK] = bq[...]
    narrow[:, 3 * RANK : 4 * RANK] = jnp.zeros((TOK, RANK), BF)
    narrow[0:16, 3 * RANK : 4 * RANK] = bv[...]

    def move(parts):
        copies = [pltpu.make_async_copy(src, out.at[:, lo:hi], sems.at[n]) for n, (src, lo, hi) in enumerate(parts)]
        for copy in copies:
            copy.start()
        for copy in copies:
            copy.wait()

    @pl.when(h_ref[0] == 0)
    def _():
        move([(wq, 256, 2304), (wo.at[:, 0:384], 2304, 2688), (narrow, 0, 256)])

    @pl.when(h_ref[0] == 1)
    def _():
        move([(wk, 0, 512), (wv, 512, 1024), (wo.at[:, 384:2048], 1024, 2688)])


def pack(*args):
    vm, anyspace = pl.BlockSpec(memory_space=pltpu.VMEM), pl.BlockSpec(memory_space=pl.ANY)
    return pl.pallas_call(
        pack_kernel,
        out_shape=jax.ShapeDtypeStruct((TOK, 2688), BF),
        in_specs=[pl.BlockSpec(memory_space=pltpu.SMEM)] + [anyspace] * 4 + [vm] * 4,
        out_specs=anyspace,
        scratch_shapes=[pltpu.VMEM((TOK, 4 * RANK), BF), pltpu.SemaphoreType.DMA((3,))],
        compiler_params=pltpu.CompilerParams(vmem_limit_bytes=16 * 2**20),
    )(*args)


def local_step(own_block, full, xa, kc, ks, bias, hid, ans, gain, sign):
    vm, anyspace = pl.BlockSpec(memory_space=pltpu.VMEM), pl.BlockSpec(memory_space=pl.ANY)
    bf, f32 = (lambda *s: pltpu.VMEM(s, BF)), (lambda *s: pltpu.VMEM(s, F32))
    return pl.pallas_call(
        local_kernel,
        out_shape=jax.ShapeDtypeStruct((8, 33, 16, 2 * RANK), BF),
        in_specs=[pl.BlockSpec(memory_space=pltpu.SMEM), anyspace] + [vm] * 8,
        out_specs=vm,
        scratch_shapes=[
            bf(D, 256), bf(D, 2 * KVW), bf(D, D), bf(D, D),
            bf(ALL, 2 * RANK), bf(KVW, 2 * RANK),
            bf(PARTS, L, HD), bf(PARTS, L, HD), bf(PARTS, L, HD),
            bf(2, PARTS, QROWS, HD), f32(PARTS, QROWS, L), bf(PARTS, QROWS, L), f32(PARTS, QROWS, HD),
            bf(2 * ROWS, D), f32(ROWS, D), bf(ROWS, D), bf(PARTS, QROWS, HD), bf(ROWS, D), bf(ALL, KVW), bf(ALL, 2 * RANK),
            pltpu.SemaphoreType.DMA((5, PIECES)),
        ],
        compiler_params=pltpu.CompilerParams(vmem_limit_bytes=50 * 2**20),
        cost_estimate=pl.CostEstimate(flops=24_000_000_000, bytes_accessed=27_000_000, transcendentals=2_100_000),
    )(own_block, full, xa, kc, ks, bias, hid, ans, gain, sign)


def body(hidden, answer_rows, resp_mask, attn_gain, final_gain, w_query, w_key, w_value, w_out, a_query, b_query, a_value, b_value):
    hidden = hidden[0]
    y_pos, h_pos = lax.axis_index("y"), lax.axis_index("h")

    h_one = jnp.full((1,), 1, jnp.int32) * h_pos
    packed = pack(h_one, w_query, w_key, w_value, w_out, a_query, a_value, b_query, b_value)
    full = lax.all_gather(packed, ("h",) + OWN, axis=0, tiled=True).reshape(2, D, packed.shape[1])

    x32 = hidden.astype(F32)
    xn = (x32 * lax.rsqrt(jnp.mean(x32 * x32, axis=-1, keepdims=True) + EPS) * attn_gain).astype(BF).reshape(ROWS, D)
    other = lax.ppermute(xn, "h", [(0, 1), (1, 0)])
    two = jnp.concatenate([xn, other], axis=0)
    every = lax.all_to_all(jnp.broadcast_to(two[None], (4,) + two.shape), "y", 0, 0, tiled=True)
    xa = every.reshape(ALL, D)

    block = jnp.arange(BLOCKS, dtype=jnp.int32)
    source = (block // 2) * 2 + jnp.bitwise_xor(block % 2, h_pos)
    token = jnp.arange(TOK, dtype=jnp.int32)
    key_pos = source[:, None] * TOK + token[None, :]
    own_pos = (y_pos * 2 + h_pos) * TOK + token
    frequency = THETA ** (-(jnp.arange(HD // 2, dtype=F32) * 2.0) / HD)
    row_pos = jnp.broadcast_to(key_pos[:, None, :], (BLOCKS, 2, TOK)).reshape(ALL)
    angles = row_pos.astype(F32)[:, None] * frequency[None, :]
    cosine, sine = jnp.cos(angles), jnp.sin(angles)
    kc = jnp.concatenate([cosine, cosine], axis=1)
    ks = jnp.concatenate([-sine, sine], axis=1)
    bias = jnp.where(own_pos[:, None] >= key_pos.reshape(1, L), 0.0, -1e30).astype(F32)
    sign = (resp_mask[0].astype(F32) * jnp.array([1.0, -1.0], F32)[:, None]).reshape(ROWS, 1)
    own_block = jnp.full((1,), 2, jnp.int32) * y_pos

    mine = local_step(own_block, full, xa, kc, ks, bias, hidden.reshape(ROWS, D), answer_rows.reshape(ROWS, D), final_gain.reshape(1, D), sign)

    seq = ("y", "h")
    got = lax.all_to_all(mine.reshape(4, 2, 33, 16, 2 * RANK), "y", 0, 0, tiled=True)
    quarter, vector = (16, 2 * RANK), jax.ShapeDtypeStruct((8, 2 * RANK), F32)
    keep, send, part = small_call(
        halves_kernel, (jax.ShapeDtypeStruct((32,) + quarter, F32), jax.ShapeDtypeStruct((33,) + quarter, BF), vector), (h_one, got), 1
    )
    met = lax.ppermute(send, "h", [(0, 1), (1, 0)])
    scaled, margin = small_call(scale_kernel, (jax.ShapeDtypeStruct((32,) + quarter, BF), vector), (keep, met, part), 0)
    shares = lax.all_to_all(scaled, OWN, 0, 0, tiled=True)
    loss = jax.nn.softplus(-BETA * margin[0, :1])
    piece = jnp.sum(shares.astype(F32), axis=0)
    total = lax.all_to_all(jnp.broadcast_to(piece[None], (8,) + piece.shape), seq, 0, 0, tiled=True)
    grad_a = total[:4].reshape(TOK, 2 * RANK)
    low_half, high_half = total[4:6, :, :RANK], total[4:6, :, RANK:]
    grad_b_q = jnp.stack([low_half, high_half], axis=1).reshape(TOK, RANK)
    return grad_a[:, :RANK], grad_b_q, grad_a[:, RANK:], total[6, :, :RANK], loss


def solution(mesh):
    fine = Mesh(mesh.devices.reshape(4, 2, 4, 2, 4), AXES)
    seq = ("y", "h")
    weights = P(OWN, None)
    in_specs = (P(OWN, None, seq, None), P(OWN, None, seq, None), P(OWN, None, seq), P(), P()) + (weights,) * 8
    out_specs = (weights,) * 4 + (P(OWN),)
    return jax.shard_map(body, mesh=fine, in_specs=in_specs, out_specs=out_specs, check_vma=False)
```

```python
import math

import jax
import jax.numpy as jnp
from jax import lax
from jax.experimental import pallas as pl
from jax.experimental.pallas import tpu as pltpu
from jax.sharding import Mesh
from jax.sharding import PartitionSpec as P

D = 2048
HQ = 16
HK = 4
HD = 128
RANK = 64
GROUP = HQ // HK
KVW = HK * HD
TOK = 64
ROWS = 2 * TOK
BLOCKS = 8
ALL = BLOCKS * ROWS
L = BLOCKS * TOK
PARTS = 2 * HK
QROWS = GROUP * TOK
PIECES = 4

EPS = 1e-05
BETA = 0.1
ADAPTER_SCALE = 2.0
THETA = 500000.0

BF = jnp.bfloat16
F32 = jnp.float32

AXES = ("z", "c", "y", "h", "x")
OWN = ("z", "c", "x")


def mm(a, b):
    return jnp.dot(a, b, preferred_element_type=F32)


def mm_t(a, b):
    return lax.dot_general(a, b, (((1,), (1,)), ((), ())), preferred_element_type=F32)


def turn(u, c, s):
    return u * c + pltpu.roll(u, HD // 2, 1) * s


def dot_rows(a, b):
    return jnp.sum(a * b, axis=-1, keepdims=True)


def split3(margin):
    lane = lax.broadcasted_iota(jnp.int32, (16, 2 * RANK), 1)
    hi = margin.astype(BF).astype(F32)
    mid = (margin - hi).astype(BF).astype(F32)
    lo = margin - hi - mid
    return jnp.where(lane == 0, hi, jnp.where(lane == 1, mid, jnp.where(lane == 2, lo, 0.0))).astype(BF)


def local_kernel(own_ref, full, xa, kc, ks, bias, hid, ans, gain, sign, out,
                 wn, wkv, wq, wo, low, bv, keys, vref, vpol, qs, prob, probb, o32, heads, yp, by, bo, bq, vt, dn, sems):
    half = D // PIECES

    def pieces(first, h, cols, dst, at):
        made = []
        for n in range(PIECES):
            rows = pl.ds(n * half, half)
            made.append(pltpu.make_async_copy(full.at[h, rows, cols[0] : cols[1]], dst.at[rows, at[0] : at[1]], sems.at[first, n]))
        return made

    copies = [
        pieces(0, 0, (0, 256), wn, (0, 256)),
        pieces(1, 1, (0, 1024), wkv, (0, 1024)),
        pieces(2, 0, (256, 2304), wq, (0, 2048)),
        pieces(3, 0, (2304, 2688), wo, (0, 384)),
        pieces(4, 1, (1024, 2688), wo, (384, 2048)),
    ]
    def begin(first):
        for copy in copies[first]:
            copy.start()

    def arrived(first):
        for copy in copies[first]:
            copy.wait()

    begin(0)
    begin(1)

    own = pl.multiple_of(own_ref[0] * ROWS, ROWS)

    arrived(0)
    lane_of = lambda n: lax.broadcasted_iota(jnp.int32, (n, 2 * RANK), 1)
    for d in range(32):
        bv[16 * d : 16 * d + 16, :] = wn[64 * d : 64 * d + 16, 2 * RANK :]
    arrived(1)
    begin(2)

    @pl.loop(0, ALL // 256, unroll=2)
    def _(r):
        r0 = pl.multiple_of(r * 256, 256)
        x = xa[pl.ds(r0, 256), :]
        lw = mm(x, wn[:, : 2 * RANK])
        low[pl.ds(r0, 256), :] = lw.astype(BF)
        c, s = kc[pl.ds(r0, 256), :], ks[pl.ds(r0, 256), :]
        kv = mm(x, wkv[...])
        lift = mm_t(jnp.where(lane_of(256) < RANK, 0.0, lw).astype(BF), bv[...])
        for g in range(HK):
            cols = slice(HD * g, HD * g + HD)
            k = turn(kv[:, cols], c, s).astype(BF)
            vr = kv[:, KVW + HD * g : KVW + HD * g + HD].astype(BF)
            vp = (vr.astype(F32) + ADAPTER_SCALE * lift[:, cols]).astype(BF)
            for b in range(2):
                t0 = pl.multiple_of(r * 2 * TOK + b * TOK, TOK)
                for side in range(2):
                    src = slice(b * ROWS + side * TOK, b * ROWS + side * TOK + TOK)
                    at = side * HK + g
                    keys[at, pl.ds(t0, TOK), :] = k[src]
                    vref[at, pl.ds(t0, TOK), :] = vr[src]
                    vpol[at, pl.ds(t0, TOK), :] = vp[src]

    arrived(2)
    begin(3)
    begin(4)
    low_own = low[pl.ds(own, ROWS), :].astype(F32)
    low_q = jnp.where(lane_of(ROWS) < RANK, low_own, 0.0).astype(BF)
    c_own, s_own = kc[pl.ds(own, ROWS), :], ks[pl.ds(own, ROWS), :]

    @pl.loop(0, HK, unroll=True)
    def _(g):
        w0 = pl.multiple_of(g * GROUP * HD, GROUP * HD)
        base = mm(xa[pl.ds(own, ROWS), :], wq[:, pl.ds(w0, GROUP * HD)])
        lift = mm_t(low_q, wn[pl.ds(w0, GROUP * HD), 2 * RANK :])
        moved = base + ADAPTER_SCALE * lift
        for j in range(GROUP):
            cols = slice(HD * j, HD * j + HD)
            qr = turn(base[:, cols], c_own, s_own).astype(BF)
            qp = turn(moved[:, cols], c_own, s_own).astype(BF)
            for side in range(2):
                src = slice(side * TOK, side * TOK + TOK)
                qs[0, side * HK + g, j * TOK : j * TOK + TOK, :] = qr[src]
                qs[1, side * HK + g, j * TOK : j * TOK + TOK, :] = qp[src]

    scale = 1.0 / math.sqrt(HD)

    def soft(q, k):
        logits = mm_t(q, k).reshape(GROUP, TOK, L) * (scale * math.log2(math.e)) + bias[...][None]
        logits = logits.reshape(QROWS, L)
        raised = jnp.exp2(logits - jnp.max(logits, axis=-1, keepdims=True))
        return raised * (1.0 / jnp.sum(raised, axis=-1, keepdims=True))

    @pl.loop(0, PARTS, unroll=4)
    def _(i):
        g, side = lax.rem(i, HK), lax.div(i, HK)
        k = keys[i]
        p0 = soft(qs[0, i], k)
        p1 = soft(qs[1, i], k)
        b1 = p1.astype(BF)
        prob[i] = p1
        probb[i] = b1
        m0 = mm(p0.astype(BF), vref[i])
        m1 = mm(b1, vpol[i])
        o32[i] = m1
        n0, n1 = m0.astype(BF), m1.astype(BF)
        r0 = pl.multiple_of(side * TOK, TOK)
        for j in range(GROUP):
            c0 = pl.multiple_of(g * GROUP * HD + j * HD, HD)
            heads[pl.ds(r0, TOK), pl.ds(c0, HD)] = n0[j * TOK : j * TOK + TOK]
            heads[pl.ds(r0 + ROWS, TOK), pl.ds(c0, HD)] = n1[j * TOK : j * TOK + TOK]

    arrived(3)
    arrived(4)
    tile = 512
    zero = jnp.zeros((ROWS, 1), F32)
    sq0, sq1, sc0, sc1 = zero, zero, zero, zero
    for n in range(D // tile):
        cols = slice(n * tile, n * tile + tile)
        y = mm(heads[...], wo[:, cols])
        x = hid[:, cols].astype(F32)
        ga = gain[:, cols] * ans[:, cols].astype(F32)
        y0, y1 = x + y[:ROWS], x + y[ROWS:]
        yp[:, cols] = y1
        sq0, sq1 = sq0 + dot_rows(y0, y0), sq1 + dot_rows(y1, y1)
        sc0, sc1 = sc0 + dot_rows(y0, ga), sc1 + dot_rows(y1, ga)
    inv0 = lax.rsqrt(sq0 * (1.0 / D) + EPS)
    inv1 = lax.rsqrt(sq1 * (1.0 / D) + EPS)
    score0, score1 = sc0 * inv0, sc1 * inv1
    sg = sign[...]
    margin = jnp.sum(sg * (score1 - score0), axis=0, keepdims=True)
    lead = inv1 * sg
    pull = inv1 * score1 * (1.0 / D)
    for n in range(D // tile):
        cols = slice(n * tile, n * tile + tile)
        ga = gain[:, cols] * ans[:, cols].astype(F32)
        by[:, cols] = (lead * (ga - yp[:, cols] * pull)).astype(BF)

    by_t = by[...].T

    @pl.loop(0, HK, unroll=True)
    def _(g):
        w0 = pl.multiple_of(g * GROUP * HD, GROUP * HD)
        back = mm(wo[pl.ds(w0, GROUP * HD), :], by_t).T.astype(BF)
        for j in range(GROUP):
            for side in range(2):
                bo[side * HK + g, j * TOK : j * TOK + TOK, :] = back[side * TOK : side * TOK + TOK, HD * j : HD * j + HD]

    @pl.loop(0, PARTS, unroll=4)
    def _(i):
        g, side = lax.rem(i, HK), lax.div(i, HK)
        b = bo[i]
        dp = mm_t(b, vpol[i])
        rd = dot_rows(b.astype(F32), o32[i]) * scale
        bl = (prob[i] * (dp * scale - rd)).astype(BF)
        dq = mm(bl, keys[i])
        term = mm(probb[i].T, b).astype(BF)
        r0 = pl.multiple_of(side * TOK, TOK)
        o0 = pl.multiple_of(own + side * TOK, TOK)
        c, s = kc[pl.ds(o0, TOK), :], ks[pl.ds(o0, TOK), :]
        for j in range(GROUP):
            c0 = pl.multiple_of(g * GROUP * HD + j * HD, HD)
            bq[pl.ds(r0, TOK), pl.ds(c0, HD)] = turn(dq[j * TOK : j * TOK + TOK], c, -s).astype(BF)
        for blk in range(BLOCKS):
            v0 = pl.multiple_of(side * TOK + blk * ROWS, TOK)
            vt[pl.ds(v0, TOK), pl.ds(pl.multiple_of(g * HD, HD), HD)] = term[blk * TOK : blk * TOK + TOK]

    dn[...] = jnp.where(lane_of(ALL) < RANK, 0.0, mm(vt[...], bv[...])).astype(BF)
    dq_low = jnp.where(lane_of(ROWS) < RANK, mm(bq[...], wn[:, 2 * RANK :]), 0.0)
    dn[pl.ds(own, ROWS), :] = (dn[pl.ds(own, ROWS), :].astype(F32) + dq_low).astype(BF)
    dn_t = dn[...].T
    low_t = low[...].T
    low_own_t = low[pl.ds(own, ROWS), :].T
    lane16 = lane_of(16)
    left = lane16 < RANK
    for n in range(D // tile):
        cols = slice(n * tile, n * tile + tile)
        ga_t = (ADAPTER_SCALE * mm(dn_t, xa[:, cols])).T
        gb_t = (ADAPTER_SCALE * mm(low_own_t, bq[:, cols])).T
        for d in range(tile // TOK):
            at = n * (tile // TOK) + d
            ga, gb = ga_t[d * TOK : d * TOK + TOK], gb_t[d * TOK : d * TOK + TOK]
            for q in range(4):
                out[q, at] = ga[q * 16 : q * 16 + 16].astype(BF)
            for q in range(2):
                out[4 + q, at] = jnp.where(left, gb[q * 32 : q * 32 + 16], pltpu.roll(gb[q * 32 + 16 : q * 32 + 32], RANK, 1)).astype(BF)
    gv_t = (ADAPTER_SCALE * mm(low_t, vt[...])).T
    for d in range(32):
        out[6, d] = jnp.where(left, pltpu.roll(gv_t[16 * d : 16 * d + 16], RANK, 1), 0.0).astype(BF)
        out[7, d] = jnp.zeros((16, 2 * RANK), BF)
    riding = split3(margin)
    for q in range(8):
        out[q, 32] = riding


def ride_of(block):
    return jnp.sum(block[0:1, :], axis=-1, keepdims=True)


def quarter_kernel(got, send):
    total = got[0].astype(F32)
    for q in range(1, 4):
        total = total + got[q].astype(F32)
    send[...] = total.astype(BF)
    ride = split3(ride_of(total[0, 32]))
    send[0, 32] = ride


def scale_kernel(sent, met, scaled, margin_out):
    margin = ride_of(sent[0, 32].astype(F32)) + ride_of(met[0, 32].astype(F32))
    margin_out[...] = jnp.broadcast_to(margin, (8, 2 * RANK))
    weight = -BETA / (1.0 + jnp.exp(BETA * margin))
    for e in range(2):
        scaled[:, e] = ((sent[e, 0:32].astype(F32) + met[e, 0:32].astype(F32)) * weight[None]).astype(BF)


def sum_kernel(shares, spread):
    total = shares[0].astype(F32)
    for q in range(1, 32):
        total = total + shares[q].astype(F32)
    for q in range(4):
        spread[q] = total


def finish_kernel(total, a_q, b_q, a_v, b_v):
    for e in range(4):
        at = slice(16 * e, 16 * e + 16)
        a_q[at, :] = total[e, :, 0:RANK]
        a_v[at, :] = total[e, :, RANK : 2 * RANK]
    for e in range(2):
        b_q[32 * e : 32 * e + 16, :] = total[4 + e, :, 0:RANK]
        b_q[32 * e + 16 : 32 * e + 32, :] = total[4 + e, :, RANK : 2 * RANK]
    b_v[...] = total[6, :, 0:RANK]


def small_call(kernel, out_shape, *args):
    vm = pl.BlockSpec(memory_space=pltpu.VMEM)
    return pl.pallas_call(
        kernel,
        out_shape=out_shape,
        in_specs=[vm] * len(args),
        out_specs=(vm,) * len(out_shape),
        compiler_params=pltpu.CompilerParams(vmem_limit_bytes=16 * 2**20),
    )(*args)


def pack_kernel(h_ref, wq, wk, wv, wo, aq, av, bq, bv, out, thin, thin_v, narrow, sems, thin_sems):
    def move(parts):
        return [pltpu.make_async_copy(src, out.at[:, lo:hi], sems.at[n]) for n, (src, lo, hi) in enumerate(parts)]

    @pl.when(h_ref[0] == 0)
    def _():
        small = [pltpu.make_async_copy(src, thin.at[n], thin_sems.at[n]) for n, src in enumerate((aq, av, bq))]
        small.append(pltpu.make_async_copy(bv, thin_v, thin_sems.at[3]))
        large = move([(wq, 256, 2304), (wo.at[:, 0:384], 2304, 2688), (narrow, 0, 256)])
        for copy in small + large[:2]:
            copy.start()
        for copy in small:
            copy.wait()
        for n in range(3):
            narrow[:, n * RANK : n * RANK + RANK] = thin[n]
        narrow[:, 3 * RANK : 4 * RANK] = jnp.zeros((TOK, RANK), BF)
        narrow[0:16, 3 * RANK : 4 * RANK] = thin_v[...]
        large[2].start()
        for copy in large:
            copy.wait()

    @pl.when(h_ref[0] == 1)
    def _():
        large = move([(wk, 0, 512), (wv, 512, 1024), (wo.at[:, 384:2048], 1024, 2688)])
        for copy in large:
            copy.start()
        for copy in large:
            copy.wait()


def pack(*args):
    anyspace = pl.BlockSpec(memory_space=pl.ANY)
    return pl.pallas_call(
        pack_kernel,
        out_shape=jax.ShapeDtypeStruct((TOK, 2688), BF),
        in_specs=[pl.BlockSpec(memory_space=pltpu.SMEM)] + [anyspace] * 8,
        out_specs=anyspace,
        scratch_shapes=[
            pltpu.VMEM((3, TOK, RANK), BF), pltpu.VMEM((16, RANK), BF), pltpu.VMEM((TOK, 4 * RANK), BF),
            pltpu.SemaphoreType.DMA((3,)), pltpu.SemaphoreType.DMA((4,)),
        ],
        compiler_params=pltpu.CompilerParams(vmem_limit_bytes=62 * 2**20),
    )(*args)


def local_step(own_block, full, xa, kc, ks, bias, hid, ans, gain, sign):
    vm, anyspace = pl.BlockSpec(memory_space=pltpu.VMEM), pl.BlockSpec(memory_space=pl.ANY)
    bf, f32 = (lambda *s: pltpu.VMEM(s, BF)), (lambda *s: pltpu.VMEM(s, F32))
    return pl.pallas_call(
        local_kernel,
        out_shape=jax.ShapeDtypeStruct((8, 33, 16, 2 * RANK), BF),
        in_specs=[pl.BlockSpec(memory_space=pltpu.SMEM), anyspace] + [vm] * 8,
        out_specs=vm,
        scratch_shapes=[
            bf(D, 256), bf(D, 2 * KVW), bf(D, D), bf(D, D),
            bf(ALL, 2 * RANK), bf(KVW, 2 * RANK),
            bf(PARTS, L, HD), bf(PARTS, L, HD), bf(PARTS, L, HD),
            bf(2, PARTS, QROWS, HD), f32(PARTS, QROWS, L), bf(PARTS, QROWS, L), f32(PARTS, QROWS, HD),
            bf(2 * ROWS, D), f32(ROWS, D), bf(ROWS, D), bf(PARTS, QROWS, HD), bf(ROWS, D), bf(ALL, KVW), bf(ALL, 2 * RANK),
            pltpu.SemaphoreType.DMA((5, PIECES)),
        ],
        compiler_params=pltpu.CompilerParams(vmem_limit_bytes=50 * 2**20),
        cost_estimate=pl.CostEstimate(flops=24_000_000_000, bytes_accessed=27_000_000, transcendentals=2_100_000),
    )(own_block, full, xa, kc, ks, bias, hid, ans, gain, sign)


def body(hidden, answer_rows, resp_mask, attn_gain, final_gain, w_query, w_key, w_value, w_out, a_query, b_query, a_value, b_value):
    hidden = hidden[0]
    y_pos, h_pos = lax.axis_index("y"), lax.axis_index("h")

    h_one = jnp.full((1,), 1, jnp.int32) * h_pos
    packed = pack(h_one, w_query, w_key, w_value, w_out, a_query, a_value, b_query, b_value)
    full = lax.all_gather(packed, ("h",) + OWN, axis=0, tiled=True).reshape(2, D, packed.shape[1])

    x32 = hidden.astype(F32)
    xn = (x32 * lax.rsqrt(jnp.mean(x32 * x32, axis=-1, keepdims=True) + EPS) * attn_gain).astype(BF).reshape(ROWS, D)
    other = lax.ppermute(xn, "h", [(0, 1), (1, 0)])
    two = jnp.concatenate([xn, other], axis=0)
    every = lax.all_to_all(jnp.broadcast_to(two[None], (4,) + two.shape), "y", 0, 0, tiled=True)
    xa = every.reshape(ALL, D)

    block = jnp.arange(BLOCKS, dtype=jnp.int32)
    source = (block // 2) * 2 + jnp.bitwise_xor(block % 2, h_pos)
    token = jnp.arange(TOK, dtype=jnp.int32)
    key_pos = source[:, None] * TOK + token[None, :]
    own_pos = (y_pos * 2 + h_pos) * TOK + token
    frequency = THETA ** (-(jnp.arange(HD // 2, dtype=F32) * 2.0) / HD)
    row_pos = jnp.broadcast_to(key_pos[:, None, :], (BLOCKS, 2, TOK)).reshape(ALL)
    angles = row_pos.astype(F32)[:, None] * frequency[None, :]
    cosine, sine = jnp.cos(angles), jnp.sin(angles)
    kc = jnp.concatenate([cosine, cosine], axis=1)
    ks = jnp.concatenate([-sine, sine], axis=1)
    bias = jnp.where(own_pos[:, None] >= key_pos.reshape(1, L), 0.0, -1e30).astype(F32)
    sign = (resp_mask[0].astype(F32) * jnp.array([1.0, -1.0], F32)[:, None]).reshape(ROWS, 1)
    own_block = jnp.full((1,), 2, jnp.int32) * y_pos

    mine = local_step(own_block, full, xa, kc, ks, bias, hidden.reshape(ROWS, D), answer_rows.reshape(ROWS, D), final_gain.reshape(1, D), sign)

    got = lax.all_to_all(mine.reshape(4, 2, 33, 16, 2 * RANK), "y", 0, 0, tiled=True)
    tile, vector = (16, 2 * RANK), jax.ShapeDtypeStruct((8, 2 * RANK), F32)
    (send,) = small_call(quarter_kernel, (jax.ShapeDtypeStruct((2, 33) + tile, BF),), got)
    met = lax.ppermute(send, "h", [(0, 1), (1, 0)])
    scaled, margin = small_call(scale_kernel, (jax.ShapeDtypeStruct((32, 2) + tile, BF), vector), send, met)
    shares = lax.all_to_all(scaled, OWN, 0, 0, tiled=True)
    loss = jax.nn.softplus(-BETA * margin[0, :1])
    (spread,) = small_call(sum_kernel, (jax.ShapeDtypeStruct((4, 2) + tile, F32),), shares)
    total = lax.all_to_all(spread, "y", 0, 0, tiled=True).reshape((8,) + tile)
    square = jax.ShapeDtypeStruct((TOK, RANK), F32)
    grads = small_call(finish_kernel, (square, square, square, jax.ShapeDtypeStruct((16, RANK), F32)), total)
    return tuple(grads) + (loss,)


def solution(mesh):
    fine = Mesh(mesh.devices.reshape(4, 2, 4, 2, 4), AXES)
    seq = ("y", "h")
    weights = P(OWN, None)
    in_specs = (P(OWN, None, seq, None), P(OWN, None, seq, None), P(OWN, None, seq), P(), P()) + (weights,) * 8
    out_specs = (weights,) * 4 + (P(OWN),)
    return jax.shard_map(body, mesh=fine, in_specs=in_specs, out_specs=out_specs, check_vma=False)
```

```python
import math

import jax
import jax.numpy as jnp
from jax import lax
from jax.experimental import pallas as pl
from jax.experimental.pallas import tpu as pltpu
from jax.sharding import Mesh
from jax.sharding import PartitionSpec as P

D = 2048
HQ = 16
HK = 4
HD = 128
RANK = 64
GROUP = HQ // HK
KVW = HK * HD
TOK = 64
ROWS = 2 * TOK
BLOCKS = 8
ALL = BLOCKS * ROWS
L = BLOCKS * TOK
PARTS = 2 * HK
QROWS = GROUP * TOK
PIECES = 4

EPS = 1e-05
BETA = 0.1
ADAPTER_SCALE = 2.0
THETA = 500000.0

BF = jnp.bfloat16
F32 = jnp.float32

AXES = ("z", "c", "y", "h", "x")
OWN = ("z", "c", "x")


def mm(a, b):
    return jnp.dot(a, b, preferred_element_type=F32)


def mm_t(a, b):
    return lax.dot_general(a, b, (((1,), (1,)), ((), ())), preferred_element_type=F32)


def turn(u, c, s):
    return u * c + pltpu.roll(u, HD // 2, 1) * s


def dot_rows(a, b):
    return jnp.sum(a * b, axis=-1, keepdims=True)


def split3(margin):
    lane = lax.broadcasted_iota(jnp.int32, (16, 2 * RANK), 1)
    hi = margin.astype(BF).astype(F32)
    mid = (margin - hi).astype(BF).astype(F32)
    lo = margin - hi - mid
    return jnp.where(lane == 0, hi, jnp.where(lane == 1, mid, jnp.where(lane == 2, lo, 0.0))).astype(BF)


def local_kernel(own_ref, full, xa, kc, ks, bias, hid, ans, gain, sign, out,
                 wn, wkv, wq, wo, low, bv, keys, vref, vpol, qs, prob, probb, o32, heads, yp, by, bo, bq, vt, dn, sems):
    half = D // PIECES

    def pieces(first, h, cols, dst, at):
        made = []
        for n in range(PIECES):
            rows = pl.ds(n * half, half)
            made.append(pltpu.make_async_copy(full.at[h, rows, cols[0] : cols[1]], dst.at[rows, at[0] : at[1]], sems.at[first, n]))
        return made

    copies = [
        pieces(0, 0, (0, 256), wn, (0, 256)),
        pieces(1, 1, (0, 1024), wkv, (0, 1024)),
        pieces(2, 0, (256, 2304), wq, (0, 2048)),
        pieces(3, 0, (2304, 2688), wo, (0, 384)),
        pieces(4, 1, (1024, 2688), wo, (384, 2048)),
    ]
    def begin(first):
        for copy in copies[first]:
            copy.start()

    def arrived(first):
        for copy in copies[first]:
            copy.wait()

    begin(0)
    begin(1)

    own = pl.multiple_of(own_ref[0] * ROWS, ROWS)

    arrived(0)
    lane_of = lambda n: lax.broadcasted_iota(jnp.int32, (n, 2 * RANK), 1)
    for d in range(32):
        bv[16 * d : 16 * d + 16, :] = wn[64 * d : 64 * d + 16, 2 * RANK :]
    arrived(1)
    begin(2)

    @pl.loop(0, ALL // 256, unroll=2)
    def _(r):
        r0 = pl.multiple_of(r * 256, 256)
        x = xa[pl.ds(r0, 256), :]
        lw = mm(x, wn[:, : 2 * RANK])
        low[pl.ds(r0, 256), :] = lw.astype(BF)
        c, s = kc[pl.ds(r0, 256), :], ks[pl.ds(r0, 256), :]
        kv = mm(x, wkv[...])
        lift = mm_t(jnp.where(lane_of(256) < RANK, 0.0, lw).astype(BF), bv[...])
        for g in range(HK):
            cols = slice(HD * g, HD * g + HD)
            k = turn(kv[:, cols], c, s).astype(BF)
            vr = kv[:, KVW + HD * g : KVW + HD * g + HD].astype(BF)
            vp = (vr.astype(F32) + ADAPTER_SCALE * lift[:, cols]).astype(BF)
            for b in range(2):
                t0 = pl.multiple_of(r * 2 * TOK + b * TOK, TOK)
                for side in range(2):
                    src = slice(b * ROWS + side * TOK, b * ROWS + side * TOK + TOK)
                    at = side * HK + g
                    keys[at, pl.ds(t0, TOK), :] = k[src]
                    vref[at, pl.ds(t0, TOK), :] = vr[src]
                    vpol[at, pl.ds(t0, TOK), :] = vp[src]

    arrived(2)
    begin(3)
    begin(4)
    low_own = low[pl.ds(own, ROWS), :].astype(F32)
    low_q = jnp.where(lane_of(ROWS) < RANK, low_own, 0.0).astype(BF)
    c_own, s_own = kc[pl.ds(own, ROWS), :], ks[pl.ds(own, ROWS), :]

    @pl.loop(0, HK, unroll=True)
    def _(g):
        w0 = pl.multiple_of(g * GROUP * HD, GROUP * HD)
        base = mm(xa[pl.ds(own, ROWS), :], wq[:, pl.ds(w0, GROUP * HD)])
        lift = mm_t(low_q, wn[pl.ds(w0, GROUP * HD), 2 * RANK :])
        moved = base + ADAPTER_SCALE * lift
        for j in range(GROUP):
            cols = slice(HD * j, HD * j + HD)
            qr = turn(base[:, cols], c_own, s_own).astype(BF)
            qp = turn(moved[:, cols], c_own, s_own).astype(BF)
            for side in range(2):
                src = slice(side * TOK, side * TOK + TOK)
                qs[0, side * HK + g, j * TOK : j * TOK + TOK, :] = qr[src]
                qs[1, side * HK + g, j * TOK : j * TOK + TOK, :] = qp[src]

    scale = 1.0 / math.sqrt(HD)

    def soft(q, k):
        logits = mm_t(q, k).reshape(GROUP, TOK, L) * (scale * math.log2(math.e)) + bias[...][None]
        logits = logits.reshape(QROWS, L)
        raised = jnp.exp2(logits - jnp.max(logits, axis=-1, keepdims=True))
        return raised * (1.0 / jnp.sum(raised, axis=-1, keepdims=True))

    @pl.loop(0, PARTS, unroll=4)
    def _(i):
        g, side = lax.rem(i, HK), lax.div(i, HK)
        k = keys[i]
        p0 = soft(qs[0, i], k)
        p1 = soft(qs[1, i], k)
        b1 = p1.astype(BF)
        prob[i] = p1
        probb[i] = b1
        m0 = mm(p0.astype(BF), vref[i])
        m1 = mm(b1, vpol[i])
        o32[i] = m1
        n0, n1 = m0.astype(BF), m1.astype(BF)
        r0 = pl.multiple_of(side * TOK, TOK)
        for j in range(GROUP):
            c0 = pl.multiple_of(g * GROUP * HD + j * HD, HD)
            heads[pl.ds(r0, TOK), pl.ds(c0, HD)] = n0[j * TOK : j * TOK + TOK]
            heads[pl.ds(r0 + ROWS, TOK), pl.ds(c0, HD)] = n1[j * TOK : j * TOK + TOK]

    arrived(3)
    arrived(4)
    tile = 512
    zero = jnp.zeros((ROWS, 1), F32)
    sq0, sq1, sc0, sc1 = zero, zero, zero, zero
    for n in range(D // tile):
        cols = slice(n * tile, n * tile + tile)
        y = mm(heads[...], wo[:, cols])
        x = hid[:, cols].astype(F32)
        ga = gain[:, cols] * ans[:, cols].astype(F32)
        y0, y1 = x + y[:ROWS], x + y[ROWS:]
        yp[:, cols] = y1
        sq0, sq1 = sq0 + dot_rows(y0, y0), sq1 + dot_rows(y1, y1)
        sc0, sc1 = sc0 + dot_rows(y0, ga), sc1 + dot_rows(y1, ga)
    inv0 = lax.rsqrt(sq0 * (1.0 / D) + EPS)
    inv1 = lax.rsqrt(sq1 * (1.0 / D) + EPS)
    score0, score1 = sc0 * inv0, sc1 * inv1
    sg = sign[...]
    margin = jnp.sum(sg * (score1 - score0), axis=0, keepdims=True)
    lead = inv1 * sg
    pull = inv1 * score1 * (1.0 / D)
    for n in range(D // tile):
        cols = slice(n * tile, n * tile + tile)
        ga = gain[:, cols] * ans[:, cols].astype(F32)
        by[:, cols] = (lead * (ga - yp[:, cols] * pull)).astype(BF)

    by_t = by[...].T

    @pl.loop(0, HK, unroll=True)
    def _(g):
        w0 = pl.multiple_of(g * GROUP * HD, GROUP * HD)
        back = mm(wo[pl.ds(w0, GROUP * HD), :], by_t).T.astype(BF)
        for j in range(GROUP):
            for side in range(2):
                bo[side * HK + g, j * TOK : j * TOK + TOK, :] = back[side * TOK : side * TOK + TOK, HD * j : HD * j + HD]

    @pl.loop(0, PARTS, unroll=4)
    def _(i):
        g, side = lax.rem(i, HK), lax.div(i, HK)
        b = bo[i]
        dp = mm_t(b, vpol[i])
        rd = dot_rows(b.astype(F32), o32[i]) * scale
        bl = (prob[i] * (dp * scale - rd)).astype(BF)
        dq = mm(bl, keys[i])
        term = mm(probb[i].T, b).astype(BF)
        r0 = pl.multiple_of(side * TOK, TOK)
        o0 = pl.multiple_of(own + side * TOK, TOK)
        c, s = kc[pl.ds(o0, TOK), :], ks[pl.ds(o0, TOK), :]
        for j in range(GROUP):
            c0 = pl.multiple_of(g * GROUP * HD + j * HD, HD)
            bq[pl.ds(r0, TOK), pl.ds(c0, HD)] = turn(dq[j * TOK : j * TOK + TOK], c, -s).astype(BF)
        for blk in range(BLOCKS):
            v0 = pl.multiple_of(side * TOK + blk * ROWS, TOK)
            vt[pl.ds(v0, TOK), pl.ds(pl.multiple_of(g * HD, HD), HD)] = term[blk * TOK : blk * TOK + TOK]

    dn[...] = jnp.where(lane_of(ALL) < RANK, 0.0, mm(vt[...], bv[...])).astype(BF)
    dq_low = jnp.where(lane_of(ROWS) < RANK, mm(bq[...], wn[:, 2 * RANK :]), 0.0)
    dn[pl.ds(own, ROWS), :] = (dn[pl.ds(own, ROWS), :].astype(F32) + dq_low).astype(BF)
    dn_t = dn[...].T
    low_t = low[...].T
    low_own_t = low[pl.ds(own, ROWS), :].T
    lane16 = lane_of(16)
    left = lane16 < RANK
    for n in range(D // tile):
        cols = slice(n * tile, n * tile + tile)
        ga_t = (ADAPTER_SCALE * mm(dn_t, xa[:, cols])).T
        gb_t = (ADAPTER_SCALE * mm(low_own_t, bq[:, cols])).T
        for d in range(tile // TOK):
            at = n * (tile // TOK) + d
            ga, gb = ga_t[d * TOK : d * TOK + TOK], gb_t[d * TOK : d * TOK + TOK]
            for q in range(4):
                out[q, at] = ga[q * 16 : q * 16 + 16].astype(BF)
            for q in range(2):
                out[4 + q, at] = jnp.where(left, gb[q * 32 : q * 32 + 16], pltpu.roll(gb[q * 32 + 16 : q * 32 + 32], RANK, 1)).astype(BF)
    gv_t = (ADAPTER_SCALE * mm(low_t, vt[...])).T
    for d in range(32):
        out[6, d] = jnp.where(left, pltpu.roll(gv_t[16 * d : 16 * d + 16], RANK, 1), 0.0).astype(BF)
        out[7, d] = jnp.zeros((16, 2 * RANK), BF)
    riding = split3(margin)
    for q in range(8):
        out[q, 32] = riding


def ride_of(block):
    return jnp.sum(block[0:1, :], axis=-1, keepdims=True)


def halves_kernel(h_ref, got, keep, send, margin_out):
    h = h_ref[0]
    ride = got[0, 0, 32].astype(F32)
    kept, sent = got[0, h, 0:32].astype(F32), got[0, 1 - h, 0:32].astype(F32)
    for q in range(1, 4):
        ride = ride + got[q, 0, 32].astype(F32)
        kept = kept + got[q, h, 0:32].astype(F32)
        sent = sent + got[q, 1 - h, 0:32].astype(F32)
    margin = ride_of(ride)
    margin_out[...] = jnp.broadcast_to(margin, (8, 2 * RANK))
    keep[...] = kept
    send[0:32] = sent.astype(BF)
    send[32] = split3(margin)


def scale_kernel(keep, met, margin_in, scaled, margin_out):
    margin = margin_in[0:1, 0:1] + ride_of(met[32].astype(F32))
    margin_out[...] = jnp.broadcast_to(margin, (8, 2 * RANK))
    weight = -BETA / (1.0 + jnp.exp(BETA * margin))
    scaled[...] = ((keep[...] + met[0:32].astype(F32)) * weight[None]).astype(BF)


def sum_kernel(shares, spread):
    total = shares[0].astype(F32)
    for q in range(1, 32):
        total = total + shares[q].astype(F32)
    for q in range(8):
        spread[q] = total


def finish_kernel(total, a_q, b_q, a_v, b_v):
    for e in range(4):
        at = slice(16 * e, 16 * e + 16)
        a_q[at, :] = total[e, :, 0:RANK]
        a_v[at, :] = total[e, :, RANK : 2 * RANK]
    for e in range(2):
        b_q[32 * e : 32 * e + 16, :] = total[4 + e, :, 0:RANK]
        b_q[32 * e + 16 : 32 * e + 32, :] = total[4 + e, :, RANK : 2 * RANK]
    b_v[...] = total[6, :, 0:RANK]


def small_call(kernel, out_shape, *args, scalars=0):
    vm = pl.BlockSpec(memory_space=pltpu.VMEM)
    return pl.pallas_call(
        kernel,
        out_shape=out_shape,
        in_specs=[pl.BlockSpec(memory_space=pltpu.SMEM)] * scalars + [vm] * (len(args) - scalars),
        out_specs=(vm,) * len(out_shape),
        compiler_params=pltpu.CompilerParams(vmem_limit_bytes=16 * 2**20),
    )(*args)


def pack_kernel(h_ref, wq, wk, wv, wo, aq, av, bq, bv, hidden, gain, out, xn, thin, thin_v, flat, hid, sems, out_sem):
    hid_copy = pltpu.make_async_copy(hidden, hid, sems.at[6])
    hid_copy.start()

    def fetch(parts):
        copies = [pltpu.make_async_copy(src, dst, sems.at[n]) for n, (src, dst) in enumerate(parts)]
        for copy in copies:
            copy.start()
        return copies

    @pl.when(h_ref[0] == 0)
    def _():
        small = [(aq, thin.at[0]), (av, thin.at[1]), (bq, thin.at[2]), (bv, thin_v)]
        copies = fetch(small + [(wq, flat.at[:, 256:2304]), (wo.at[:, 0:384], flat.at[:, 2304:2688])])
        for copy in copies[:4]:
            copy.wait()
        for n in range(3):
            flat[:, n * RANK : n * RANK + RANK] = thin[n]
        flat[:, 3 * RANK : 4 * RANK] = jnp.zeros((TOK, RANK), BF)
        flat[0:16, 3 * RANK : 4 * RANK] = thin_v[...]
        for copy in copies[4:]:
            copy.wait()

    @pl.when(h_ref[0] == 1)
    def _():
        for copy in fetch([(wk, flat.at[:, 0:512]), (wv, flat.at[:, 512:1024]), (wo.at[:, 384:2048], flat.at[:, 1024:2688])]):
            copy.wait()

    done = pltpu.make_async_copy(flat, out, out_sem)
    done.start()
    hid_copy.wait()
    x = hid[...].astype(F32)
    xn[...] = (x * lax.rsqrt(jnp.mean(x * x, axis=-1, keepdims=True) + EPS) * gain[...]).astype(BF)
    done.wait()


def pack(*args):
    vm, anyspace = pl.BlockSpec(memory_space=pltpu.VMEM), pl.BlockSpec(memory_space=pl.ANY)
    return pl.pallas_call(
        pack_kernel,
        out_shape=(jax.ShapeDtypeStruct((TOK, 2688), BF), jax.ShapeDtypeStruct((ROWS, D), BF)),
        in_specs=[pl.BlockSpec(memory_space=pltpu.SMEM)] + [anyspace] * 9 + [vm],
        out_specs=(anyspace, vm),
        scratch_shapes=[
            pltpu.VMEM((3, TOK, RANK), BF), pltpu.VMEM((16, RANK), BF), pltpu.VMEM((TOK, 2688), BF), pltpu.VMEM((ROWS, D), BF),
            pltpu.SemaphoreType.DMA((7,)), pltpu.SemaphoreType.DMA,
        ],
        compiler_params=pltpu.CompilerParams(vmem_limit_bytes=60 * 2**20),
    )(*args)


def local_step(own_block, full, xa, kc, ks, bias, hid, ans, gain, sign):
    vm, anyspace = pl.BlockSpec(memory_space=pltpu.VMEM), pl.BlockSpec(memory_space=pl.ANY)
    bf, f32 = (lambda *s: pltpu.VMEM(s, BF)), (lambda *s: pltpu.VMEM(s, F32))
    return pl.pallas_call(
        local_kernel,
        out_shape=jax.ShapeDtypeStruct((8, 33, 16, 2 * RANK), BF),
        in_specs=[pl.BlockSpec(memory_space=pltpu.SMEM), anyspace] + [vm] * 8,
        out_specs=vm,
        scratch_shapes=[
            bf(D, 256), bf(D, 2 * KVW), bf(D, D), bf(D, D),
            bf(ALL, 2 * RANK), bf(KVW, 2 * RANK),
            bf(PARTS, L, HD), bf(PARTS, L, HD), bf(PARTS, L, HD),
            bf(2, PARTS, QROWS, HD), f32(PARTS, QROWS, L), bf(PARTS, QROWS, L), f32(PARTS, QROWS, HD),
            bf(2 * ROWS, D), f32(ROWS, D), bf(ROWS, D), bf(PARTS, QROWS, HD), bf(ROWS, D), bf(ALL, KVW), bf(ALL, 2 * RANK),
            pltpu.SemaphoreType.DMA((5, PIECES)),
        ],
        compiler_params=pltpu.CompilerParams(vmem_limit_bytes=50 * 2**20),
        cost_estimate=pl.CostEstimate(flops=24_000_000_000, bytes_accessed=27_000_000, transcendentals=2_100_000),
    )(own_block, full, xa, kc, ks, bias, hid, ans, gain, sign)


def body(hidden, answer_rows, resp_mask, attn_gain, final_gain, w_query, w_key, w_value, w_out, a_query, b_query, a_value, b_value):
    hidden = hidden[0]
    y_pos, h_pos = lax.axis_index("y"), lax.axis_index("h")

    h_one = jnp.full((1,), 1, jnp.int32) * h_pos
    packed, xn = pack(
        h_one, w_query, w_key, w_value, w_out, a_query, a_value, b_query, b_value, hidden.reshape(ROWS, D), attn_gain.reshape(1, D)
    )
    other = lax.ppermute(xn, "h", [(0, 1), (1, 0)])
    full = lax.all_gather(packed, ("h",) + OWN, axis=0, tiled=True).reshape(2, D, packed.shape[1])

    two = jnp.concatenate([xn, other], axis=0)
    every = lax.all_to_all(jnp.broadcast_to(two[None], (4,) + two.shape), "y", 0, 0, tiled=True)
    xa = every.reshape(ALL, D)

    block = jnp.arange(BLOCKS, dtype=jnp.int32)
    source = (block // 2) * 2 + jnp.bitwise_xor(block % 2, h_pos)
    token = jnp.arange(TOK, dtype=jnp.int32)
    key_pos = source[:, None] * TOK + token[None, :]
    own_pos = (y_pos * 2 + h_pos) * TOK + token
    frequency = THETA ** (-(jnp.arange(HD // 2, dtype=F32) * 2.0) / HD)
    row_pos = jnp.broadcast_to(key_pos[:, None, :], (BLOCKS, 2, TOK)).reshape(ALL)
    angles = row_pos.astype(F32)[:, None] * frequency[None, :]
    cosine, sine = jnp.cos(angles), jnp.sin(angles)
    kc = jnp.concatenate([cosine, cosine], axis=1)
    ks = jnp.concatenate([-sine, sine], axis=1)
    bias = jnp.where(own_pos[:, None] >= key_pos.reshape(1, L), 0.0, -1e30).astype(F32)
    sign = (resp_mask[0].astype(F32) * jnp.array([1.0, -1.0], F32)[:, None]).reshape(ROWS, 1)
    own_block = jnp.full((1,), 2, jnp.int32) * y_pos

    mine = local_step(own_block, full, xa, kc, ks, bias, hidden.reshape(ROWS, D), answer_rows.reshape(ROWS, D), final_gain.reshape(1, D), sign)

    got = lax.all_to_all(mine.reshape(4, 2, 33, 16, 2 * RANK), "y", 0, 0, tiled=True)
    tile, vector = (16, 2 * RANK), jax.ShapeDtypeStruct((8, 2 * RANK), F32)
    keep, send, part = small_call(
        halves_kernel, (jax.ShapeDtypeStruct((32,) + tile, F32), jax.ShapeDtypeStruct((33,) + tile, BF), vector), h_one, got, scalars=1
    )
    met = lax.ppermute(send, "h", [(0, 1), (1, 0)])
    scaled, margin = small_call(scale_kernel, (jax.ShapeDtypeStruct((32,) + tile, BF), vector), keep, met, part)
    shares = lax.all_to_all(scaled, OWN, 0, 0, tiled=True)
    loss = jax.nn.softplus(-BETA * margin[0, :1])
    (spread,) = small_call(sum_kernel, (jax.ShapeDtypeStruct((8,) + tile, F32),), shares)
    total = lax.all_to_all(spread, ("y", "h"), 0, 0, tiled=True)
    square = jax.ShapeDtypeStruct((TOK, RANK), F32)
    grads = small_call(finish_kernel, (square, square, square, jax.ShapeDtypeStruct((16, RANK), F32)), total)
    return tuple(grads) + (loss,)


def solution(mesh):
    fine = Mesh(mesh.devices.reshape(4, 2, 4, 2, 4), AXES)
    seq = ("y", "h")
    weights = P(OWN, None)
    in_specs = (P(OWN, None, seq, None), P(OWN, None, seq, None), P(OWN, None, seq), P(), P()) + (weights,) * 8
    out_specs = (weights,) * 4 + (P(OWN),)
    return jax.shard_map(body, mesh=fine, in_specs=in_specs, out_specs=out_specs, check_vma=False)
```

```python
import math

import jax
import jax.numpy as jnp
from jax import lax
from jax.experimental import pallas as pl
from jax.experimental.pallas import tpu as pltpu
from jax.sharding import Mesh
from jax.sharding import PartitionSpec as P

D = 2048
HQ = 16
HK = 4
HD = 128
RANK = 64
GROUP = HQ // HK
KVW = HK * HD
TOK = 64
ROWS = 2 * TOK
BLOCKS = 8
ALL = BLOCKS * ROWS
L = BLOCKS * TOK
PARTS = 2 * HK
QROWS = GROUP * TOK
PIECES = 4

EPS = 1e-05
BETA = 0.1
ADAPTER_SCALE = 2.0
THETA = 500000.0

BF = jnp.bfloat16
F32 = jnp.float32

AXES = ("z", "c", "y", "h", "x")
OWN = ("z", "c", "x")


def mm(a, b):
    return jnp.dot(a, b, preferred_element_type=F32)


def mm_t(a, b):
    return lax.dot_general(a, b, (((1,), (1,)), ((), ())), preferred_element_type=F32)


def turn(u, c, s):
    return u * c + pltpu.roll(u, HD // 2, 1) * s


def dot_rows(a, b):
    return jnp.sum(a * b, axis=-1, keepdims=True)


def split3(margin):
    lane = lax.broadcasted_iota(jnp.int32, (16, 2 * RANK), 1)
    hi = margin.astype(BF).astype(F32)
    mid = (margin - hi).astype(BF).astype(F32)
    lo = margin - hi - mid
    return jnp.where(lane == 0, hi, jnp.where(lane == 1, mid, jnp.where(lane == 2, lo, 0.0))).astype(BF)


def local_kernel(own_ref, full, xa, kc, ks, bias, hid, ans, gain, sign, out,
                 wn, wkv, wq, wo, low, bv, keys, vref, vpol, qs, prob, probb, o32, heads, yp, by, bo, bq, vt, dn, sems):
    half = D // PIECES

    def pieces(first, h, cols, dst, at):
        made = []
        for n in range(PIECES):
            rows = pl.ds(n * half, half)
            made.append(pltpu.make_async_copy(full.at[h, rows, cols[0] : cols[1]], dst.at[rows, at[0] : at[1]], sems.at[first, n]))
        return made

    copies = [
        pieces(0, 0, (0, 256), wn, (0, 256)),
        pieces(1, 1, (0, 1024), wkv, (0, 1024)),
        pieces(2, 0, (256, 2304), wq, (0, 2048)),
        pieces(3, 0, (2304, 2688), wo, (0, 384)),
        pieces(4, 1, (1024, 2688), wo, (384, 2048)),
    ]
    def begin(first):
        for copy in copies[first]:
            copy.start()

    def arrived(first):
        for copy in copies[first]:
            copy.wait()

    begin(0)
    begin(1)

    own = pl.multiple_of(own_ref[0] * ROWS, ROWS)

    arrived(0)
    lane_of = lambda n: lax.broadcasted_iota(jnp.int32, (n, 2 * RANK), 1)
    for d in range(32):
        bv[16 * d : 16 * d + 16, :] = wn[64 * d : 64 * d + 16, 2 * RANK :]
    arrived(1)
    begin(2)

    @pl.loop(0, ALL // 256, unroll=2)
    def _(r):
        r0 = pl.multiple_of(r * 256, 256)
        x = xa[pl.ds(r0, 256), :]
        lw = mm(x, wn[:, : 2 * RANK])
        low[pl.ds(r0, 256), :] = lw.astype(BF)
        c, s = kc[pl.ds(r0, 256), :], ks[pl.ds(r0, 256), :]
        kv = mm(x, wkv[...])
        lift = mm_t(jnp.where(lane_of(256) < RANK, 0.0, lw).astype(BF), bv[...])
        for g in range(HK):
            cols = slice(HD * g, HD * g + HD)
            k = turn(kv[:, cols], c, s).astype(BF)
            vr = kv[:, KVW + HD * g : KVW + HD * g + HD].astype(BF)
            vp = (vr.astype(F32) + ADAPTER_SCALE * lift[:, cols]).astype(BF)
            for b in range(2):
                t0 = pl.multiple_of(r * 2 * TOK + b * TOK, TOK)
                for side in range(2):
                    src = slice(b * ROWS + side * TOK, b * ROWS + side * TOK + TOK)
                    at = side * HK + g
                    keys[at, pl.ds(t0, TOK), :] = k[src]
                    vref[at, pl.ds(t0, TOK), :] = vr[src]
                    vpol[at, pl.ds(t0, TOK), :] = vp[src]

    arrived(2)
    begin(3)
    begin(4)
    low_own = low[pl.ds(own, ROWS), :].astype(F32)
    low_q = jnp.where(lane_of(ROWS) < RANK, low_own, 0.0).astype(BF)
    c_own, s_own = kc[pl.ds(own, ROWS), :], ks[pl.ds(own, ROWS), :]

    @pl.loop(0, HK, unroll=True)
    def _(g):
        w0 = pl.multiple_of(g * GROUP * HD, GROUP * HD)
        base = mm(xa[pl.ds(own, ROWS), :], wq[:, pl.ds(w0, GROUP * HD)])
        lift = mm_t(low_q, wn[pl.ds(w0, GROUP * HD), 2 * RANK :])
        moved = base + ADAPTER_SCALE * lift
        for j in range(GROUP):
            cols = slice(HD * j, HD * j + HD)
            qr = turn(base[:, cols], c_own, s_own).astype(BF)
            qp = turn(moved[:, cols], c_own, s_own).astype(BF)
            for side in range(2):
                src = slice(side * TOK, side * TOK + TOK)
                qs[0, side * HK + g, j * TOK : j * TOK + TOK, :] = qr[src]
                qs[1, side * HK + g, j * TOK : j * TOK + TOK, :] = qp[src]

    scale = 1.0 / math.sqrt(HD)

    def soft(q, k):
        logits = mm_t(q, k).reshape(GROUP, TOK, L) * (scale * math.log2(math.e)) + bias[...][None]
        logits = logits.reshape(QROWS, L)
        raised = jnp.exp2(logits - jnp.max(logits, axis=-1, keepdims=True))
        return raised * (1.0 / jnp.sum(raised, axis=-1, keepdims=True))

    @pl.loop(0, PARTS, unroll=4)
    def _(i):
        g, side = lax.rem(i, HK), lax.div(i, HK)
        k = keys[i]
        p0 = soft(qs[0, i], k)
        p1 = soft(qs[1, i], k)
        b1 = p1.astype(BF)
        prob[i] = p1
        probb[i] = b1
        m0 = mm(p0.astype(BF), vref[i])
        m1 = mm(b1, vpol[i])
        o32[i] = m1
        n0, n1 = m0.astype(BF), m1.astype(BF)
        r0 = pl.multiple_of(side * TOK, TOK)
        for j in range(GROUP):
            c0 = pl.multiple_of(g * GROUP * HD + j * HD, HD)
            heads[pl.ds(r0, TOK), pl.ds(c0, HD)] = n0[j * TOK : j * TOK + TOK]
            heads[pl.ds(r0 + ROWS, TOK), pl.ds(c0, HD)] = n1[j * TOK : j * TOK + TOK]

    arrived(3)
    arrived(4)
    tile = 512
    zero = jnp.zeros((ROWS, 1), F32)
    sq0, sq1, sc0, sc1 = zero, zero, zero, zero
    for n in range(D // tile):
        cols = slice(n * tile, n * tile + tile)
        y = mm(heads[...], wo[:, cols])
        x = hid[:, cols].astype(F32)
        ga = gain[:, cols] * ans[:, cols].astype(F32)
        y0, y1 = x + y[:ROWS], x + y[ROWS:]
        yp[:, cols] = y1
        sq0, sq1 = sq0 + dot_rows(y0, y0), sq1 + dot_rows(y1, y1)
        sc0, sc1 = sc0 + dot_rows(y0, ga), sc1 + dot_rows(y1, ga)
    inv0 = lax.rsqrt(sq0 * (1.0 / D) + EPS)
    inv1 = lax.rsqrt(sq1 * (1.0 / D) + EPS)
    score0, score1 = sc0 * inv0, sc1 * inv1
    sg = sign[...]
    margin = jnp.sum(sg * (score1 - score0), axis=0, keepdims=True)
    lead = inv1 * sg
    pull = inv1 * score1 * (1.0 / D)
    for n in range(D // tile):
        cols = slice(n * tile, n * tile + tile)
        ga = gain[:, cols] * ans[:, cols].astype(F32)
        by[:, cols] = (lead * (ga - yp[:, cols] * pull)).astype(BF)

    by_t = by[...].T

    @pl.loop(0, HK, unroll=True)
    def _(g):
        w0 = pl.multiple_of(g * GROUP * HD, GROUP * HD)
        back = mm(wo[pl.ds(w0, GROUP * HD), :], by_t).T.astype(BF)
        for j in range(GROUP):
            for side in range(2):
                bo[side * HK + g, j * TOK : j * TOK + TOK, :] = back[side * TOK : side * TOK + TOK, HD * j : HD * j + HD]

    @pl.loop(0, PARTS, unroll=4)
    def _(i):
        g, side = lax.rem(i, HK), lax.div(i, HK)
        b = bo[i]
        dp = mm_t(b, vpol[i])
        rd = dot_rows(b.astype(F32), o32[i]) * scale
        bl = (prob[i] * (dp * scale - rd)).astype(BF)
        dq = mm(bl, keys[i])
        term = mm(probb[i].T, b).astype(BF)
        r0 = pl.multiple_of(side * TOK, TOK)
        o0 = pl.multiple_of(own + side * TOK, TOK)
        c, s = kc[pl.ds(o0, TOK), :], ks[pl.ds(o0, TOK), :]
        for j in range(GROUP):
            c0 = pl.multiple_of(g * GROUP * HD + j * HD, HD)
            bq[pl.ds(r0, TOK), pl.ds(c0, HD)] = turn(dq[j * TOK : j * TOK + TOK], c, -s).astype(BF)
        for blk in range(BLOCKS):
            v0 = pl.multiple_of(side * TOK + blk * ROWS, TOK)
            vt[pl.ds(v0, TOK), pl.ds(pl.multiple_of(g * HD, HD), HD)] = term[blk * TOK : blk * TOK + TOK]

    dn[...] = jnp.where(lane_of(ALL) < RANK, 0.0, mm(vt[...], bv[...])).astype(BF)
    dq_low = jnp.where(lane_of(ROWS) < RANK, mm(bq[...], wn[:, 2 * RANK :]), 0.0)
    dn[pl.ds(own, ROWS), :] = (dn[pl.ds(own, ROWS), :].astype(F32) + dq_low).astype(BF)
    dn_t = dn[...].T
    low_t = low[...].T
    low_own_t = low[pl.ds(own, ROWS), :].T
    left = lane_of(8) < RANK
    for n in range(D // tile):
        cols = slice(n * tile, n * tile + tile)
        ga = (ADAPTER_SCALE * mm(dn_t, xa[:, cols])).astype(BF).T
        gb = (ADAPTER_SCALE * mm(low_own_t, bq[:, cols])).T
        for d in range(tile // TOK):
            for q in range(4):
                r0 = d * TOK + 16 * q
                out[q, n * (tile // TOK) + d] = ga[r0 : r0 + 16]
        for pair in range(tile // TOK // 2):
            for q in range(4):
                both = []
                for r0 in (2 * pair * TOK + 16 * q, (2 * pair + 1) * TOK + 16 * q):
                    both.append(jnp.where(left, gb[r0 : r0 + 8], pltpu.roll(gb[r0 + 8 : r0 + 16], RANK, 1)))
                out[q, 32 + n * (tile // TOK // 2) + pair] = jnp.concatenate(both, axis=0).astype(BF)
    gv = (ADAPTER_SCALE * mm(low_t, vt[...])).T
    for quad in range(8):
        for q in range(2):
            v = [gv[16 * (4 * quad + j) + 8 * q : 16 * (4 * quad + j) + 8 * q + 8] for j in range(4)]
            both = [jnp.where(left, pltpu.roll(v[j], RANK, 1), v[j + 1]) for j in (0, 2)]
            out[q, 48 + quad] = jnp.concatenate(both, axis=0).astype(BF)
            out[2 + q, 48 + quad] = jnp.zeros((16, 2 * RANK), BF)
    riding = split3(margin)
    for q in range(4):
        out[q, 56] = riding


def ride_of(block):
    return jnp.sum(block[0:1, :], axis=-1, keepdims=True)


def halves_kernel(h_ref, got, keep, send, margin_out, both):
    h = h_ref[0]
    total = got[0].astype(F32)
    for q in range(1, 4):
        total = total + got[q].astype(F32)
    left = lax.broadcasted_iota(jnp.int32, (8, 2 * RANK), 1) < RANK
    for d in range(32):
        b0, v0 = 8 * (d % 2), 8 * (d % 4 // 2)
        b = total[32 + d // 2, b0 : b0 + 8]
        v = total[48 + d // 4, v0 : v0 + 8]
        if d % 2 == 0:
            v = pltpu.roll(v, RANK, 1)
        both[0, d, 0:8] = total[d, 0:8]
        both[0, d, 8:16] = jnp.where(left, b, v)
        both[1, d, 0:8] = total[d, 8:16]
        both[1, d, 8:16] = jnp.where(left, pltpu.roll(b, RANK, 1), 0.0)
    margin = ride_of(total[56])
    margin_out[...] = jnp.broadcast_to(margin, (8, 2 * RANK))
    keep[...] = both[h]
    send[0:32] = both[1 - h].astype(BF)
    send[32] = split3(margin)


def scale_kernel(keep, met, margin_in, scaled, margin_out):
    margin = margin_in[0:1, 0:1] + ride_of(met[32].astype(F32))
    margin_out[...] = jnp.broadcast_to(margin, (8, 2 * RANK))
    weight = -BETA / (1.0 + jnp.exp(BETA * margin))
    scaled[...] = ((keep[...] + met[0:32].astype(F32)) * weight[None]).astype(BF)


def sum_kernel(shares, spread):
    total = shares[0].astype(F32)
    for q in range(1, 32):
        total = total + shares[q].astype(F32)
    for q in range(8):
        spread[q] = total


def finish_kernel(total, a_q, b_q, a_v, b_v):
    for e in range(8):
        at = slice(8 * e, 8 * e + 8)
        a_q[at, :] = total[e, 0:8, 0:RANK]
        a_v[at, :] = total[e, 0:8, RANK : 2 * RANK]
        b_q[at, :] = total[e, 8:16, 0:RANK]
    for q in range(2):
        b_v[8 * q : 8 * q + 8, :] = total[2 * q, 8:16, RANK : 2 * RANK]


def small_call(kernel, out_shape, *args, scalars=0, scratch=()):
    vm = pl.BlockSpec(memory_space=pltpu.VMEM)
    return pl.pallas_call(
        kernel,
        out_shape=out_shape,
        in_specs=[pl.BlockSpec(memory_space=pltpu.SMEM)] * scalars + [vm] * (len(args) - scalars),
        out_specs=(vm,) * len(out_shape),
        scratch_shapes=scratch,
        compiler_params=pltpu.CompilerParams(vmem_limit_bytes=16 * 2**20),
    )(*args)


def pack_kernel(h_ref, wq, wk, wv, wo, aq, av, bq, bv, hidden, gain, out, xn, thin, thin_v, flat, hid, sems, out_sem):
    hid_copy = pltpu.make_async_copy(hidden, hid, sems.at[6])
    hid_copy.start()

    def fetch(parts):
        copies = [pltpu.make_async_copy(src, dst, sems.at[n]) for n, (src, dst) in enumerate(parts)]
        for copy in copies:
            copy.start()
        return copies

    @pl.when(h_ref[0] == 0)
    def _():
        small = [(aq, thin.at[0]), (av, thin.at[1]), (bq, thin.at[2]), (bv, thin_v)]
        copies = fetch(small + [(wq, flat.at[:, 256:2304]), (wo.at[:, 0:384], flat.at[:, 2304:2688])])
        for copy in copies[:4]:
            copy.wait()
        for n in range(3):
            flat[:, n * RANK : n * RANK + RANK] = thin[n]
        flat[:, 3 * RANK : 4 * RANK] = jnp.zeros((TOK, RANK), BF)
        flat[0:16, 3 * RANK : 4 * RANK] = thin_v[...]
        for copy in copies[4:]:
            copy.wait()

    @pl.when(h_ref[0] == 1)
    def _():
        for copy in fetch([(wk, flat.at[:, 0:512]), (wv, flat.at[:, 512:1024]), (wo.at[:, 384:2048], flat.at[:, 1024:2688])]):
            copy.wait()

    done = pltpu.make_async_copy(flat, out, out_sem)
    done.start()
    hid_copy.wait()
    x = hid[...].astype(F32)
    xn[...] = (x * lax.rsqrt(jnp.mean(x * x, axis=-1, keepdims=True) + EPS) * gain[...]).astype(BF)
    done.wait()


def pack(*args):
    vm, anyspace = pl.BlockSpec(memory_space=pltpu.VMEM), pl.BlockSpec(memory_space=pl.ANY)
    return pl.pallas_call(
        pack_kernel,
        out_shape=(jax.ShapeDtypeStruct((TOK, 2688), BF), jax.ShapeDtypeStruct((ROWS, D), BF)),
        in_specs=[pl.BlockSpec(memory_space=pltpu.SMEM)] + [anyspace] * 9 + [vm],
        out_specs=(anyspace, vm),
        scratch_shapes=[
            pltpu.VMEM((3, TOK, RANK), BF), pltpu.VMEM((16, RANK), BF), pltpu.VMEM((TOK, 2688), BF), pltpu.VMEM((ROWS, D), BF),
            pltpu.SemaphoreType.DMA((7,)), pltpu.SemaphoreType.DMA,
        ],
        compiler_params=pltpu.CompilerParams(vmem_limit_bytes=60 * 2**20),
    )(*args)


def local_step(own_block, full, xa, kc, ks, bias, hid, ans, gain, sign):
    vm, anyspace = pl.BlockSpec(memory_space=pltpu.VMEM), pl.BlockSpec(memory_space=pl.ANY)
    bf, f32 = (lambda *s: pltpu.VMEM(s, BF)), (lambda *s: pltpu.VMEM(s, F32))
    return pl.pallas_call(
        local_kernel,
        out_shape=jax.ShapeDtypeStruct((4, 57, 16, 2 * RANK), BF),
        in_specs=[pl.BlockSpec(memory_space=pltpu.SMEM), anyspace] + [vm] * 8,
        out_specs=vm,
        scratch_shapes=[
            bf(D, 256), bf(D, 2 * KVW), bf(D, D), bf(D, D),
            bf(ALL, 2 * RANK), bf(KVW, 2 * RANK),
            bf(PARTS, L, HD), bf(PARTS, L, HD), bf(PARTS, L, HD),
            bf(2, PARTS, QROWS, HD), f32(PARTS, QROWS, L), bf(PARTS, QROWS, L), f32(PARTS, QROWS, HD),
            bf(2 * ROWS, D), f32(ROWS, D), bf(ROWS, D), bf(PARTS, QROWS, HD), bf(ROWS, D), bf(ALL, KVW), bf(ALL, 2 * RANK),
            pltpu.SemaphoreType.DMA((5, PIECES)),
        ],
        compiler_params=pltpu.CompilerParams(vmem_limit_bytes=50 * 2**20),
        cost_estimate=pl.CostEstimate(flops=24_000_000_000, bytes_accessed=27_000_000, transcendentals=2_100_000),
    )(own_block, full, xa, kc, ks, bias, hid, ans, gain, sign)


def body(hidden, answer_rows, resp_mask, attn_gain, final_gain, w_query, w_key, w_value, w_out, a_query, b_query, a_value, b_value):
    hidden = hidden[0]
    y_pos, h_pos = lax.axis_index("y"), lax.axis_index("h")

    h_one = jnp.full((1,), 1, jnp.int32) * h_pos
    packed, xn = pack(
        h_one, w_query, w_key, w_value, w_out, a_query, a_value, b_query, b_value, hidden.reshape(ROWS, D), attn_gain.reshape(1, D)
    )
    other = lax.ppermute(xn, "h", [(0, 1), (1, 0)])
    full = lax.all_gather(packed, ("h",) + OWN, axis=0, tiled=True).reshape(2, D, packed.shape[1])

    two = jnp.concatenate([xn, other], axis=0)
    every = lax.all_to_all(jnp.broadcast_to(two[None], (4,) + two.shape), "y", 0, 0, tiled=True)
    xa = every.reshape(ALL, D)

    block = jnp.arange(BLOCKS, dtype=jnp.int32)
    source = (block // 2) * 2 + jnp.bitwise_xor(block % 2, h_pos)
    token = jnp.arange(TOK, dtype=jnp.int32)
    key_pos = source[:, None] * TOK + token[None, :]
    own_pos = (y_pos * 2 + h_pos) * TOK + token
    frequency = THETA ** (-(jnp.arange(HD // 2, dtype=F32) * 2.0) / HD)
    row_pos = jnp.broadcast_to(key_pos[:, None, :], (BLOCKS, 2, TOK)).reshape(ALL)
    angles = row_pos.astype(F32)[:, None] * frequency[None, :]
    cosine, sine = jnp.cos(angles), jnp.sin(angles)
    kc = jnp.concatenate([cosine, cosine], axis=1)
    ks = jnp.concatenate([-sine, sine], axis=1)
    bias = jnp.where(own_pos[:, None] >= key_pos.reshape(1, L), 0.0, -1e30).astype(F32)
    sign = (resp_mask[0].astype(F32) * jnp.array([1.0, -1.0], F32)[:, None]).reshape(ROWS, 1)
    own_block = jnp.full((1,), 2, jnp.int32) * y_pos

    mine = local_step(own_block, full, xa, kc, ks, bias, hidden.reshape(ROWS, D), answer_rows.reshape(ROWS, D), final_gain.reshape(1, D), sign)

    got = lax.all_to_all(mine, "y", 0, 0, tiled=True)
    tile, vector = (16, 2 * RANK), jax.ShapeDtypeStruct((8, 2 * RANK), F32)
    keep, send, part = small_call(
        halves_kernel, (jax.ShapeDtypeStruct((32,) + tile, F32), jax.ShapeDtypeStruct((33,) + tile, BF), vector), h_one, got, scalars=1,
        scratch=(pltpu.VMEM((2, 32) + tile, F32),),
    )
    met = lax.ppermute(send, "h", [(0, 1), (1, 0)])
    scaled, margin = small_call(scale_kernel, (jax.ShapeDtypeStruct((32,) + tile, BF), vector), keep, met, part)
    shares = lax.all_to_all(scaled, OWN, 0, 0, tiled=True)
    loss = jax.nn.softplus(-BETA * margin[0, :1])
    (spread,) = small_call(sum_kernel, (jax.ShapeDtypeStruct((8,) + tile, F32),), shares)
    total = lax.all_to_all(spread, ("y", "h"), 0, 0, tiled=True)
    square = jax.ShapeDtypeStruct((TOK, RANK), F32)
    grads = small_call(finish_kernel, (square, square, square, jax.ShapeDtypeStruct((16, RANK), F32)), total)
    return tuple(grads) + (loss,)


def solution(mesh):
    fine = Mesh(mesh.devices.reshape(4, 2, 4, 2, 4), AXES)
    seq = ("y", "h")
    weights = P(OWN, None)
    in_specs = (P(OWN, None, seq, None), P(OWN, None, seq, None), P(OWN, None, seq), P(), P()) + (weights,) * 8
    out_specs = (weights,) * 4 + (P(OWN),)
    return jax.shard_map(body, mesh=fine, in_specs=in_specs, out_specs=out_specs, check_vma=False)
```

```python
import math

import jax
import jax.numpy as jnp
from jax import lax
from jax.experimental import pallas as pl
from jax.experimental.pallas import tpu as pltpu
from jax.sharding import Mesh
from jax.sharding import PartitionSpec as P

D = 2048
HQ = 16
HK = 4
HD = 128
RANK = 64
GROUP = HQ // HK
KVW = HK * HD
TOK = 64
ROWS = 2 * TOK
BLOCKS = 8
ALL = BLOCKS * ROWS
L = BLOCKS * TOK
PARTS = 2 * HK
QROWS = GROUP * TOK
PIECES = 4

EPS = 1e-05
BETA = 0.1
ADAPTER_SCALE = 2.0
THETA = 500000.0

BF = jnp.bfloat16
F32 = jnp.float32

AXES = ("z", "c", "y", "h", "x")
OWN = ("z", "c", "x")


def mm(a, b):
    return jnp.dot(a, b, preferred_element_type=F32)


def mm_t(a, b):
    return lax.dot_general(a, b, (((1,), (1,)), ((), ())), preferred_element_type=F32)


def turn(u, c, s):
    return u * c + pltpu.roll(u, HD // 2, 1) * s


def dot_rows(a, b):
    return jnp.sum(a * b, axis=-1, keepdims=True)


def split3(margin):
    lane = lax.broadcasted_iota(jnp.int32, (16, 2 * RANK), 1)
    hi = margin.astype(BF).astype(F32)
    mid = (margin - hi).astype(BF).astype(F32)
    lo = margin - hi - mid
    return jnp.where(lane == 0, hi, jnp.where(lane == 1, mid, jnp.where(lane == 2, lo, 0.0))).astype(BF)


def local_kernel(own_ref, full, xa, kc, ks, bias, hid, ans, gain, sign, out,
                 wn, wkv, wq, wo, low, bv, keys, vref, vpol, qs, prob, probb, o32, heads, yp, by, bo, bq, vt, dn, sems):
    half = D // PIECES

    def pieces(first, h, cols, dst, at):
        made = []
        for n in range(PIECES):
            rows = pl.ds(n * half, half)
            made.append(pltpu.make_async_copy(full.at[h, rows, cols[0] : cols[1]], dst.at[rows, at[0] : at[1]], sems.at[first, n]))
        return made

    copies = [
        pieces(0, 1, (0, KVW), wkv, (0, KVW)),
        pieces(1, 0, (0, 256), wn, (0, 256)) + pieces(5, 1, (KVW, 2 * KVW), wkv, (KVW, 2 * KVW)),
        pieces(2, 0, (256, 2304), wq, (0, 2048)),
        pieces(3, 0, (2304, 2688), wo, (0, 384)),
        pieces(4, 1, (1024, 2688), wo, (384, 2048)),
    ]
    def begin(first):
        for copy in copies[first]:
            copy.start()

    def arrived(first):
        for copy in copies[first]:
            copy.wait()

    begin(0)
    begin(1)
    begin(2)

    own = pl.multiple_of(own_ref[0] * ROWS, ROWS)

    lane_of = lambda n: lax.broadcasted_iota(jnp.int32, (n, 2 * RANK), 1)
    arrived(0)

    def spread_rows(ref, g, r, value):
        for b in range(2):
            t0 = pl.multiple_of(r * 2 * TOK + b * TOK, TOK)
            for side in range(2):
                ref[side * HK + g, pl.ds(t0, TOK), :] = value[b * ROWS + side * TOK : b * ROWS + side * TOK + TOK]

    @pl.loop(0, ALL // 256, unroll=2)
    def _(r):
        r0 = pl.multiple_of(r * 256, 256)
        c, s = kc[pl.ds(r0, 256), :], ks[pl.ds(r0, 256), :]
        k = mm(xa[pl.ds(r0, 256), :], wkv[:, :KVW])
        for g in range(HK):
            spread_rows(keys, g, r, turn(k[:, HD * g : HD * g + HD], c, s).astype(BF))

    arrived(1)
    for d in range(32):
        bv[16 * d : 16 * d + 16, :] = wn[64 * d : 64 * d + 16, 2 * RANK :]

    @pl.loop(0, ALL // 256, unroll=2)
    def _(r):
        r0 = pl.multiple_of(r * 256, 256)
        x = xa[pl.ds(r0, 256), :]
        lw = mm(x, wn[:, : 2 * RANK])
        low[pl.ds(r0, 256), :] = lw.astype(BF)
        v = mm(x, wkv[:, KVW:])
        lift = mm_t(jnp.where(lane_of(256) < RANK, 0.0, lw).astype(BF), bv[...])
        for g in range(HK):
            cols = slice(HD * g, HD * g + HD)
            vr = v[:, cols].astype(BF)
            spread_rows(vref, g, r, vr)
            spread_rows(vpol, g, r, (vr.astype(F32) + ADAPTER_SCALE * lift[:, cols]).astype(BF))

    arrived(2)
    begin(3)
    begin(4)
    low_own = low[pl.ds(own, ROWS), :].astype(F32)
    low_q = jnp.where(lane_of(ROWS) < RANK, low_own, 0.0).astype(BF)
    c_own, s_own = kc[pl.ds(own, ROWS), :], ks[pl.ds(own, ROWS), :]

    @pl.loop(0, HK, unroll=True)
    def _(g):
        w0 = pl.multiple_of(g * GROUP * HD, GROUP * HD)
        base = mm(xa[pl.ds(own, ROWS), :], wq[:, pl.ds(w0, GROUP * HD)])
        lift = mm_t(low_q, wn[pl.ds(w0, GROUP * HD), 2 * RANK :])
        moved = base + ADAPTER_SCALE * lift
        for j in range(GROUP):
            cols = slice(HD * j, HD * j + HD)
            qr = turn(base[:, cols], c_own, s_own).astype(BF)
            qp = turn(moved[:, cols], c_own, s_own).astype(BF)
            for side in range(2):
                src = slice(side * TOK, side * TOK + TOK)
                qs[0, side * HK + g, j * TOK : j * TOK + TOK, :] = qr[src]
                qs[1, side * HK + g, j * TOK : j * TOK + TOK, :] = qp[src]

    scale = 1.0 / math.sqrt(HD)

    def soft(q, k):
        logits = mm_t(q, k).reshape(GROUP, TOK, L) * (scale * math.log2(math.e)) + bias[...][None]
        logits = logits.reshape(QROWS, L)
        raised = jnp.exp2(logits - jnp.max(logits, axis=-1, keepdims=True))
        return raised * (1.0 / jnp.sum(raised, axis=-1, keepdims=True))

    @pl.loop(0, PARTS, unroll=4)
    def _(i):
        g, side = lax.rem(i, HK), lax.div(i, HK)
        k = keys[i]
        p0 = soft(qs[0, i], k)
        p1 = soft(qs[1, i], k)
        b1 = p1.astype(BF)
        prob[i] = p1
        probb[i] = b1
        m0 = mm(p0.astype(BF), vref[i])
        m1 = mm(b1, vpol[i])
        o32[i] = m1
        n0, n1 = m0.astype(BF), m1.astype(BF)
        r0 = pl.multiple_of(side * TOK, TOK)
        for j in range(GROUP):
            c0 = pl.multiple_of(g * GROUP * HD + j * HD, HD)
            heads[pl.ds(r0, TOK), pl.ds(c0, HD)] = n0[j * TOK : j * TOK + TOK]
            heads[pl.ds(r0 + ROWS, TOK), pl.ds(c0, HD)] = n1[j * TOK : j * TOK + TOK]

    arrived(3)
    arrived(4)
    tile = 512
    zero = jnp.zeros((ROWS, 1), F32)
    sq0, sq1, sc0, sc1 = zero, zero, zero, zero
    for n in range(D // tile):
        cols = slice(n * tile, n * tile + tile)
        y = mm(heads[...], wo[:, cols])
        x = hid[:, cols].astype(F32)
        ga = gain[:, cols] * ans[:, cols].astype(F32)
        y0, y1 = x + y[:ROWS], x + y[ROWS:]
        yp[:, cols] = y1
        sq0, sq1 = sq0 + dot_rows(y0, y0), sq1 + dot_rows(y1, y1)
        sc0, sc1 = sc0 + dot_rows(y0, ga), sc1 + dot_rows(y1, ga)
    inv0 = lax.rsqrt(sq0 * (1.0 / D) + EPS)
    inv1 = lax.rsqrt(sq1 * (1.0 / D) + EPS)
    score0, score1 = sc0 * inv0, sc1 * inv1
    sg = sign[...]
    margin = jnp.sum(sg * (score1 - score0), axis=0, keepdims=True)
    lead = inv1 * sg
    pull = inv1 * score1 * (1.0 / D)
    for n in range(D // tile):
        cols = slice(n * tile, n * tile + tile)
        ga = gain[:, cols] * ans[:, cols].astype(F32)
        by[:, cols] = (lead * (ga - yp[:, cols] * pull)).astype(BF)

    by_t = by[...].T

    @pl.loop(0, HK, unroll=True)
    def _(g):
        w0 = pl.multiple_of(g * GROUP * HD, GROUP * HD)
        back = mm(wo[pl.ds(w0, GROUP * HD), :], by_t).T.astype(BF)
        for j in range(GROUP):
            for side in range(2):
                bo[side * HK + g, j * TOK : j * TOK + TOK, :] = back[side * TOK : side * TOK + TOK, HD * j : HD * j + HD]

    @pl.loop(0, PARTS, unroll=4)
    def _(i):
        g, side = lax.rem(i, HK), lax.div(i, HK)
        b = bo[i]
        dp = mm_t(b, vpol[i])
        rd = dot_rows(b.astype(F32), o32[i]) * scale
        bl = (prob[i] * (dp * scale - rd)).astype(BF)
        dq = mm(bl, keys[i])
        term = mm(probb[i].T, b).astype(BF)
        r0 = pl.multiple_of(side * TOK, TOK)
        o0 = pl.multiple_of(own + side * TOK, TOK)
        c, s = kc[pl.ds(o0, TOK), :], ks[pl.ds(o0, TOK), :]
        for j in range(GROUP):
            c0 = pl.multiple_of(g * GROUP * HD + j * HD, HD)
            bq[pl.ds(r0, TOK), pl.ds(c0, HD)] = turn(dq[j * TOK : j * TOK + TOK], c, -s).astype(BF)
        for blk in range(BLOCKS):
            v0 = pl.multiple_of(side * TOK + blk * ROWS, TOK)
            vt[pl.ds(v0, TOK), pl.ds(pl.multiple_of(g * HD, HD), HD)] = term[blk * TOK : blk * TOK + TOK]

    dn[...] = jnp.where(lane_of(ALL) < RANK, 0.0, mm(vt[...], bv[...])).astype(BF)
    dq_low = jnp.where(lane_of(ROWS) < RANK, mm(bq[...], wn[:, 2 * RANK :]), 0.0)
    dn[pl.ds(own, ROWS), :] = (dn[pl.ds(own, ROWS), :].astype(F32) + dq_low).astype(BF)
    dn_t = dn[...].T
    low_t = low[...].T
    low_own_t = low[pl.ds(own, ROWS), :].T
    left = lane_of(8) < RANK
    for n in range(D // tile):
        cols = slice(n * tile, n * tile + tile)
        ga = (ADAPTER_SCALE * mm(dn_t, xa[:, cols])).astype(BF).T
        gb = (ADAPTER_SCALE * mm(low_own_t, bq[:, cols])).T
        for d in range(tile // TOK):
            for q in range(4):
                r0 = d * TOK + 16 * q
                out[q, n * (tile // TOK) + d] = ga[r0 : r0 + 16]
        for pair in range(tile // TOK // 2):
            for q in range(4):
                both = []
                for r0 in (2 * pair * TOK + 16 * q, (2 * pair + 1) * TOK + 16 * q):
                    both.append(jnp.where(left, gb[r0 : r0 + 8], pltpu.roll(gb[r0 + 8 : r0 + 16], RANK, 1)))
                out[q, 32 + n * (tile // TOK // 2) + pair] = jnp.concatenate(both, axis=0).astype(BF)
    gv = (ADAPTER_SCALE * mm(low_t, vt[...])).T
    for quad in range(8):
        for q in range(2):
            v = [gv[16 * (4 * quad + j) + 8 * q : 16 * (4 * quad + j) + 8 * q + 8] for j in range(4)]
            both = [jnp.where(left, pltpu.roll(v[j], RANK, 1), v[j + 1]) for j in (0, 2)]
            out[q, 48 + quad] = jnp.concatenate(both, axis=0).astype(BF)
            out[2 + q, 48 + quad] = jnp.zeros((16, 2 * RANK), BF)
    riding = split3(margin)
    for q in range(4):
        out[q, 56] = riding


def ride_of(block):
    return jnp.sum(block[0:1, :], axis=-1, keepdims=True)


def halves_kernel(h_ref, got, keep, send, margin_out, both):
    h = h_ref[0]
    total = got[0].astype(F32)
    for q in range(1, 4):
        total = total + got[q].astype(F32)
    left = lax.broadcasted_iota(jnp.int32, (8, 2 * RANK), 1) < RANK
    for d in range(32):
        b0, v0 = 8 * (d % 2), 8 * (d % 4 // 2)
        b = total[32 + d // 2, b0 : b0 + 8]
        v = total[48 + d // 4, v0 : v0 + 8]
        if d % 2 == 0:
            v = pltpu.roll(v, RANK, 1)
        both[0, d, 0:8] = total[d, 0:8]
        both[0, d, 8:16] = jnp.where(left, b, v)
        both[1, d, 0:8] = total[d, 8:16]
        both[1, d, 8:16] = jnp.where(left, pltpu.roll(b, RANK, 1), 0.0)
    margin = ride_of(total[56])
    margin_out[...] = jnp.broadcast_to(margin, (8, 2 * RANK))
    keep[...] = both[h]
    send[0:32] = both[1 - h].astype(BF)
    send[32] = split3(margin)


def scale_kernel(keep, met, margin_in, scaled, margin_out):
    margin = margin_in[0:1, 0:1] + ride_of(met[32].astype(F32))
    margin_out[...] = jnp.broadcast_to(margin, (8, 2 * RANK))
    weight = -BETA / (1.0 + jnp.exp(BETA * margin))
    scaled[...] = ((keep[...] + met[0:32].astype(F32)) * weight[None]).astype(BF)


def sum_kernel(shares, spread):
    total = shares[0].astype(F32)
    for q in range(1, 32):
        total = total + shares[q].astype(F32)
    for q in range(8):
        spread[q] = total


def finish_kernel(total, a_q, b_q, a_v, b_v):
    for e in range(8):
        at = slice(8 * e, 8 * e + 8)
        a_q[at, :] = total[e, 0:8, 0:RANK]
        a_v[at, :] = total[e, 0:8, RANK : 2 * RANK]
        b_q[at, :] = total[e, 8:16, 0:RANK]
    for q in range(2):
        b_v[8 * q : 8 * q + 8, :] = total[2 * q, 8:16, RANK : 2 * RANK]


def small_call(kernel, out_shape, *args, scalars=0, scratch=()):
    vm = pl.BlockSpec(memory_space=pltpu.VMEM)
    return pl.pallas_call(
        kernel,
        out_shape=out_shape,
        in_specs=[pl.BlockSpec(memory_space=pltpu.SMEM)] * scalars + [vm] * (len(args) - scalars),
        out_specs=(vm,) * len(out_shape),
        scratch_shapes=scratch,
        compiler_params=pltpu.CompilerParams(vmem_limit_bytes=16 * 2**20),
    )(*args)


def pack_kernel(h_ref, wq, wk, wv, wo, aq, av, bq, bv, hidden, gain, out, xn, thin, thin_v, flat, hid, sems, out_sem):
    hid_copy = pltpu.make_async_copy(hidden, hid, sems.at[6])
    hid_copy.start()

    def fetch(parts):
        copies = [pltpu.make_async_copy(src, dst, sems.at[n]) for n, (src, dst) in enumerate(parts)]
        for copy in copies:
            copy.start()
        return copies

    @pl.when(h_ref[0] == 0)
    def _():
        small = [(aq, thin.at[0]), (av, thin.at[1]), (bq, thin.at[2]), (bv, thin_v)]
        copies = fetch(small + [(wq, flat.at[:, 256:2304]), (wo.at[:, 0:384], flat.at[:, 2304:2688])])
        for copy in copies[:4]:
            copy.wait()
        for n in range(3):
            flat[:, n * RANK : n * RANK + RANK] = thin[n]
        flat[:, 3 * RANK : 4 * RANK] = jnp.zeros((TOK, RANK), BF)
        flat[0:16, 3 * RANK : 4 * RANK] = thin_v[...]
        for copy in copies[4:]:
            copy.wait()

    @pl.when(h_ref[0] == 1)
    def _():
        for copy in fetch([(wk, flat.at[:, 0:512]), (wv, flat.at[:, 512:1024]), (wo.at[:, 384:2048], flat.at[:, 1024:2688])]):
            copy.wait()

    done = pltpu.make_async_copy(flat, out, out_sem)
    done.start()
    hid_copy.wait()
    x = hid[...].astype(F32)
    xn[...] = (x * lax.rsqrt(jnp.mean(x * x, axis=-1, keepdims=True) + EPS) * gain[...]).astype(BF)
    done.wait()


def pack(*args):
    vm, anyspace = pl.BlockSpec(memory_space=pltpu.VMEM), pl.BlockSpec(memory_space=pl.ANY)
    return pl.pallas_call(
        pack_kernel,
        out_shape=(jax.ShapeDtypeStruct((TOK, 2688), BF), jax.ShapeDtypeStruct((ROWS, D), BF)),
        in_specs=[pl.BlockSpec(memory_space=pltpu.SMEM)] + [anyspace] * 9 + [vm],
        out_specs=(anyspace, vm),
        scratch_shapes=[
            pltpu.VMEM((3, TOK, RANK), BF), pltpu.VMEM((16, RANK), BF), pltpu.VMEM((TOK, 2688), BF), pltpu.VMEM((ROWS, D), BF),
            pltpu.SemaphoreType.DMA((7,)), pltpu.SemaphoreType.DMA,
        ],
        compiler_params=pltpu.CompilerParams(vmem_limit_bytes=60 * 2**20),
    )(*args)


def local_step(own_block, full, xa, kc, ks, bias, hid, ans, gain, sign):
    vm, anyspace = pl.BlockSpec(memory_space=pltpu.VMEM), pl.BlockSpec(memory_space=pl.ANY)
    bf, f32 = (lambda *s: pltpu.VMEM(s, BF)), (lambda *s: pltpu.VMEM(s, F32))
    return pl.pallas_call(
        local_kernel,
        out_shape=jax.ShapeDtypeStruct((4, 57, 16, 2 * RANK), BF),
        in_specs=[pl.BlockSpec(memory_space=pltpu.SMEM), anyspace] + [vm] * 8,
        out_specs=vm,
        scratch_shapes=[
            bf(D, 256), bf(D, 2 * KVW), bf(D, D), bf(D, D),
            bf(ALL, 2 * RANK), bf(KVW, 2 * RANK),
            bf(PARTS, L, HD), bf(PARTS, L, HD), bf(PARTS, L, HD),
            bf(2, PARTS, QROWS, HD), f32(PARTS, QROWS, L), bf(PARTS, QROWS, L), f32(PARTS, QROWS, HD),
            bf(2 * ROWS, D), f32(ROWS, D), bf(ROWS, D), bf(PARTS, QROWS, HD), bf(ROWS, D), bf(ALL, KVW), bf(ALL, 2 * RANK),
            pltpu.SemaphoreType.DMA((6, PIECES)),
        ],
        compiler_params=pltpu.CompilerParams(vmem_limit_bytes=50 * 2**20),
        cost_estimate=pl.CostEstimate(flops=24_000_000_000, bytes_accessed=27_000_000, transcendentals=2_100_000),
    )(own_block, full, xa, kc, ks, bias, hid, ans, gain, sign)


def body(hidden, answer_rows, resp_mask, attn_gain, final_gain, w_query, w_key, w_value, w_out, a_query, b_query, a_value, b_value):
    hidden = hidden[0]
    y_pos, h_pos = lax.axis_index("y"), lax.axis_index("h")

    h_one = jnp.full((1,), 1, jnp.int32) * h_pos
    packed, xn = pack(
        h_one, w_query, w_key, w_value, w_out, a_query, a_value, b_query, b_value, hidden.reshape(ROWS, D), attn_gain.reshape(1, D)
    )
    other = lax.ppermute(xn, "h", [(0, 1), (1, 0)])
    full = lax.all_gather(packed, ("h",) + OWN, axis=0, tiled=True).reshape(2, D, packed.shape[1])

    two = jnp.concatenate([xn, other], axis=0)
    every = lax.all_to_all(jnp.broadcast_to(two[None], (4,) + two.shape), "y", 0, 0, tiled=True)
    xa = every.reshape(ALL, D)

    block = jnp.arange(BLOCKS, dtype=jnp.int32)
    source = (block // 2) * 2 + jnp.bitwise_xor(block % 2, h_pos)
    token = jnp.arange(TOK, dtype=jnp.int32)
    key_pos = source[:, None] * TOK + token[None, :]
    own_pos = (y_pos * 2 + h_pos) * TOK + token
    frequency = THETA ** (-(jnp.arange(HD // 2, dtype=F32) * 2.0) / HD)
    row_pos = jnp.broadcast_to(key_pos[:, None, :], (BLOCKS, 2, TOK)).reshape(ALL)
    angles = row_pos.astype(F32)[:, None] * frequency[None, :]
    cosine, sine = jnp.cos(angles), jnp.sin(angles)
    kc = jnp.concatenate([cosine, cosine], axis=1)
    ks = jnp.concatenate([-sine, sine], axis=1)
    bias = jnp.where(own_pos[:, None] >= key_pos.reshape(1, L), 0.0, -1e30).astype(F32)
    sign = (resp_mask[0].astype(F32) * jnp.array([1.0, -1.0], F32)[:, None]).reshape(ROWS, 1)
    own_block = jnp.full((1,), 2, jnp.int32) * y_pos

    mine = local_step(own_block, full, xa, kc, ks, bias, hidden.reshape(ROWS, D), answer_rows.reshape(ROWS, D), final_gain.reshape(1, D), sign)

    got = lax.all_to_all(mine, "y", 0, 0, tiled=True)
    tile, vector = (16, 2 * RANK), jax.ShapeDtypeStruct((8, 2 * RANK), F32)
    keep, send, part = small_call(
        halves_kernel, (jax.ShapeDtypeStruct((32,) + tile, F32), jax.ShapeDtypeStruct((33,) + tile, BF), vector), h_one, got, scalars=1,
        scratch=(pltpu.VMEM((2, 32) + tile, F32),),
    )
    met = lax.ppermute(send, "h", [(0, 1), (1, 0)])
    scaled, margin = small_call(scale_kernel, (jax.ShapeDtypeStruct((32,) + tile, BF), vector), keep, met, part)
    shares = lax.all_to_all(scaled, OWN, 0, 0, tiled=True)
    loss = jax.nn.softplus(-BETA * margin[0, :1])
    (spread,) = small_call(sum_kernel, (jax.ShapeDtypeStruct((8,) + tile, F32),), shares)
    total = lax.all_to_all(spread, ("y", "h"), 0, 0, tiled=True)
    square = jax.ShapeDtypeStruct((TOK, RANK), F32)
    grads = small_call(finish_kernel, (square, square, square, jax.ShapeDtypeStruct((16, RANK), F32)), total)
    return tuple(grads) + (loss,)


def solution(mesh):
    fine = Mesh(mesh.devices.reshape(4, 2, 4, 2, 4), AXES)
    seq = ("y", "h")
    weights = P(OWN, None)
    in_specs = (P(OWN, None, seq, None), P(OWN, None, seq, None), P(OWN, None, seq), P(), P()) + (weights,) * 8
    out_specs = (weights,) * 4 + (P(OWN),)
    return jax.shard_map(body, mesh=fine, in_specs=in_specs, out_specs=out_specs, check_vma=False)
```

```python
import math

import jax
import jax.numpy as jnp
from jax import lax
from jax.experimental import pallas as pl
from jax.experimental.pallas import tpu as pltpu
from jax.sharding import Mesh
from jax.sharding import PartitionSpec as P

D = 2048
HQ = 16
HK = 4
HD = 128
RANK = 64
GROUP = HQ // HK
KVW = HK * HD
TOK = 64
ROWS = 2 * TOK
BLOCKS = 8
ALL = BLOCKS * ROWS
L = BLOCKS * TOK
PARTS = 2 * HK
QROWS = GROUP * TOK
PIECES = 4

EPS = 1e-05
BETA = 0.1
ADAPTER_SCALE = 2.0
THETA = 500000.0

BF = jnp.bfloat16
F32 = jnp.float32

AXES = ("z", "c", "y", "h", "x")
OWN = ("z", "c", "x")


def mm(a, b):
    return jnp.dot(a, b, preferred_element_type=F32)


def mm_t(a, b):
    return lax.dot_general(a, b, (((1,), (1,)), ((), ())), preferred_element_type=F32)


def turn(u, c, s):
    return u * c + pltpu.roll(u, HD // 2, 1) * s


def dot_rows(a, b):
    return jnp.sum(a * b, axis=-1, keepdims=True)


def split3(margin):
    lane = lax.broadcasted_iota(jnp.int32, (16, 2 * RANK), 1)
    hi = margin.astype(BF).astype(F32)
    mid = (margin - hi).astype(BF).astype(F32)
    lo = margin - hi - mid
    return jnp.where(lane == 0, hi, jnp.where(lane == 1, mid, jnp.where(lane == 2, lo, 0.0))).astype(BF)


def local_kernel(own_ref, full, xa, kc, ks, bias, hid, ans, gain, sign, out,
                 wn, wkv, wq, wo, low, bv, keys, vref, vpol, qs, prob, probb, o32, heads, yp, by, bo, bq, vt, dn, sems):
    half = D // PIECES

    def pieces(first, h, cols, dst, at):
        made = []
        for n in range(PIECES):
            rows = pl.ds(n * half, half)
            made.append(pltpu.make_async_copy(full.at[h, rows, cols[0] : cols[1]], dst.at[rows, at[0] : at[1]], sems.at[first, n]))
        return made

    copies = [
        pieces(0, 1, (0, KVW), wkv, (0, KVW)),
        pieces(1, 0, (0, 256), wn, (0, 256)) + pieces(5, 1, (KVW, 2 * KVW), wkv, (KVW, 2 * KVW)),
        pieces(2, 0, (256, 2304), wq, (0, 2048)),
        pieces(3, 0, (2304, 2688), wo, (0, 384)),
        pieces(4, 1, (1024, 2688), wo, (384, 2048)),
    ]
    def begin(first):
        for copy in copies[first]:
            copy.start()

    def arrived(first):
        for copy in copies[first]:
            copy.wait()

    begin(0)
    begin(1)
    begin(2)

    own = pl.multiple_of(own_ref[0] * ROWS, ROWS)

    lane_of = lambda n: lax.broadcasted_iota(jnp.int32, (n, 2 * RANK), 1)
    arrived(0)

    def spread_rows(ref, g, r, value):
        for b in range(2):
            t0 = pl.multiple_of(r * 2 * TOK + b * TOK, TOK)
            for side in range(2):
                ref[side * HK + g, pl.ds(t0, TOK), :] = value[b * ROWS + side * TOK : b * ROWS + side * TOK + TOK]

    @pl.loop(0, ALL // 256, unroll=4)
    def _(r):
        r0 = pl.multiple_of(r * 256, 256)
        c, s = kc[pl.ds(r0, 256), :], ks[pl.ds(r0, 256), :]
        k = mm(xa[pl.ds(r0, 256), :], wkv[:, :KVW])
        for g in range(HK):
            spread_rows(keys, g, r, turn(k[:, HD * g : HD * g + HD], c, s).astype(BF))

    arrived(1)
    for d in range(32):
        bv[16 * d : 16 * d + 16, :] = wn[64 * d : 64 * d + 16, 2 * RANK :]

    @pl.loop(0, ALL // 256, unroll=4)
    def _(r):
        r0 = pl.multiple_of(r * 256, 256)
        x = xa[pl.ds(r0, 256), :]
        lw = mm(x, wn[:, : 2 * RANK])
        low[pl.ds(r0, 256), :] = lw.astype(BF)
        v = mm(x, wkv[:, KVW:])
        lift = mm_t(jnp.where(lane_of(256) < RANK, 0.0, lw).astype(BF), bv[...])
        for g in range(HK):
            cols = slice(HD * g, HD * g + HD)
            vr = v[:, cols].astype(BF)
            spread_rows(vref, g, r, vr)
            spread_rows(vpol, g, r, (vr.astype(F32) + ADAPTER_SCALE * lift[:, cols]).astype(BF))

    arrived(2)
    begin(3)
    begin(4)
    low_own = low[pl.ds(own, ROWS), :].astype(F32)
    low_q = jnp.where(lane_of(ROWS) < RANK, low_own, 0.0).astype(BF)
    c_own, s_own = kc[pl.ds(own, ROWS), :], ks[pl.ds(own, ROWS), :]

    @pl.loop(0, HK, unroll=True)
    def _(g):
        w0 = pl.multiple_of(g * GROUP * HD, GROUP * HD)
        base = mm(xa[pl.ds(own, ROWS), :], wq[:, pl.ds(w0, GROUP * HD)])
        lift = mm_t(low_q, wn[pl.ds(w0, GROUP * HD), 2 * RANK :])
        moved = base + ADAPTER_SCALE * lift
        for j in range(GROUP):
            cols = slice(HD * j, HD * j + HD)
            qr = turn(base[:, cols], c_own, s_own).astype(BF)
            qp = turn(moved[:, cols], c_own, s_own).astype(BF)
            for side in range(2):
                src = slice(side * TOK, side * TOK + TOK)
                qs[0, side * HK + g, j * TOK : j * TOK + TOK, :] = qr[src]
                qs[1, side * HK + g, j * TOK : j * TOK + TOK, :] = qp[src]

    scale = 1.0 / math.sqrt(HD)

    def soft(q, k):
        logits = mm_t(q, k).reshape(GROUP, TOK, L) * (scale * math.log2(math.e)) + bias[...][None]
        logits = logits.reshape(QROWS, L)
        raised = jnp.exp2(logits - jnp.max(logits, axis=-1, keepdims=True))
        return raised * (1.0 / jnp.sum(raised, axis=-1, keepdims=True))

    @pl.loop(0, PARTS, unroll=4)
    def _(i):
        g, side = lax.rem(i, HK), lax.div(i, HK)
        k = keys[i]
        p0 = soft(qs[0, i], k)
        p1 = soft(qs[1, i], k)
        b1 = p1.astype(BF)
        prob[i] = p1
        probb[i] = b1
        m0 = mm(p0.astype(BF), vref[i])
        m1 = mm(b1, vpol[i])
        o32[i] = m1
        n0, n1 = m0.astype(BF), m1.astype(BF)
        r0 = pl.multiple_of(side * TOK, TOK)
        for j in range(GROUP):
            c0 = pl.multiple_of(g * GROUP * HD + j * HD, HD)
            heads[pl.ds(r0, TOK), pl.ds(c0, HD)] = n0[j * TOK : j * TOK + TOK]
            heads[pl.ds(r0 + ROWS, TOK), pl.ds(c0, HD)] = n1[j * TOK : j * TOK + TOK]

    arrived(3)
    arrived(4)
    tile = 512
    zero = jnp.zeros((ROWS, 1), F32)
    sq0, sq1, sc0, sc1 = zero, zero, zero, zero
    for n in range(D // tile):
        cols = slice(n * tile, n * tile + tile)
        y = mm(heads[...], wo[:, cols])
        x = hid[:, cols].astype(F32)
        ga = gain[:, cols] * ans[:, cols].astype(F32)
        y0, y1 = x + y[:ROWS], x + y[ROWS:]
        yp[:, cols] = y1
        sq0, sq1 = sq0 + dot_rows(y0, y0), sq1 + dot_rows(y1, y1)
        sc0, sc1 = sc0 + dot_rows(y0, ga), sc1 + dot_rows(y1, ga)
    inv0 = lax.rsqrt(sq0 * (1.0 / D) + EPS)
    inv1 = lax.rsqrt(sq1 * (1.0 / D) + EPS)
    score0, score1 = sc0 * inv0, sc1 * inv1
    sg = sign[...]
    margin = jnp.sum(sg * (score1 - score0), axis=0, keepdims=True)
    lead = inv1 * sg
    pull = inv1 * score1 * (1.0 / D)
    for n in range(D // tile):
        cols = slice(n * tile, n * tile + tile)
        ga = gain[:, cols] * ans[:, cols].astype(F32)
        by[:, cols] = (lead * (ga - yp[:, cols] * pull)).astype(BF)

    by_t = by[...].T

    @pl.loop(0, HK, unroll=True)
    def _(g):
        w0 = pl.multiple_of(g * GROUP * HD, GROUP * HD)
        back = mm(wo[pl.ds(w0, GROUP * HD), :], by_t).T.astype(BF)
        for j in range(GROUP):
            for side in range(2):
                bo[side * HK + g, j * TOK : j * TOK + TOK, :] = back[side * TOK : side * TOK + TOK, HD * j : HD * j + HD]

    @pl.loop(0, PARTS, unroll=4)
    def _(i):
        g, side = lax.rem(i, HK), lax.div(i, HK)
        b = bo[i]
        dp = mm_t(b, vpol[i])
        rd = dot_rows(b.astype(F32), o32[i]) * scale
        bl = (prob[i] * (dp * scale - rd)).astype(BF)
        dq = mm(bl, keys[i])
        term = mm(probb[i].T, b).astype(BF)
        r0 = pl.multiple_of(side * TOK, TOK)
        o0 = pl.multiple_of(own + side * TOK, TOK)
        c, s = kc[pl.ds(o0, TOK), :], ks[pl.ds(o0, TOK), :]
        for j in range(GROUP):
            c0 = pl.multiple_of(g * GROUP * HD + j * HD, HD)
            bq[pl.ds(r0, TOK), pl.ds(c0, HD)] = turn(dq[j * TOK : j * TOK + TOK], c, -s).astype(BF)
        for blk in range(BLOCKS):
            v0 = pl.multiple_of(side * TOK + blk * ROWS, TOK)
            vt[pl.ds(v0, TOK), pl.ds(pl.multiple_of(g * HD, HD), HD)] = term[blk * TOK : blk * TOK + TOK]

    dn[...] = jnp.where(lane_of(ALL) < RANK, 0.0, mm(vt[...], bv[...])).astype(BF)
    dq_low = jnp.where(lane_of(ROWS) < RANK, mm(bq[...], wn[:, 2 * RANK :]), 0.0)
    dn[pl.ds(own, ROWS), :] = (dn[pl.ds(own, ROWS), :].astype(F32) + dq_low).astype(BF)
    dn_t = dn[...].T
    low_t = low[...].T
    low_own_t = low[pl.ds(own, ROWS), :].T
    left = lane_of(8) < RANK
    for n in range(D // tile):
        cols = slice(n * tile, n * tile + tile)
        ga = (ADAPTER_SCALE * mm(dn_t, xa[:, cols])).astype(BF).T
        gb = (ADAPTER_SCALE * mm(low_own_t, bq[:, cols])).T
        for d in range(tile // TOK):
            for q in range(4):
                r0 = d * TOK + 16 * q
                out[q, n * (tile // TOK) + d] = ga[r0 : r0 + 16]
        for pair in range(tile // TOK // 2):
            for q in range(4):
                both = []
                for r0 in (2 * pair * TOK + 16 * q, (2 * pair + 1) * TOK + 16 * q):
                    both.append(jnp.where(left, gb[r0 : r0 + 8], pltpu.roll(gb[r0 + 8 : r0 + 16], RANK, 1)))
                out[q, 32 + n * (tile // TOK // 2) + pair] = jnp.concatenate(both, axis=0).astype(BF)
    gv = (ADAPTER_SCALE * mm(low_t, vt[...])).T
    for quad in range(8):
        for q in range(2):
            v = [gv[16 * (4 * quad + j) + 8 * q : 16 * (4 * quad + j) + 8 * q + 8] for j in range(4)]
            both = [jnp.where(left, pltpu.roll(v[j], RANK, 1), v[j + 1]) for j in (0, 2)]
            out[q, 48 + quad] = jnp.concatenate(both, axis=0).astype(BF)
            out[2 + q, 48 + quad] = jnp.zeros((16, 2 * RANK), BF)
    riding = split3(margin)
    for q in range(4):
        out[q, 56] = riding


def ride_of(block):
    return jnp.sum(block[0:1, :], axis=-1, keepdims=True)


def halves_kernel(h_ref, got, keep, send, margin_out, both):
    h = h_ref[0]
    total = got[0].astype(F32)
    for q in range(1, 4):
        total = total + got[q].astype(F32)
    left = lax.broadcasted_iota(jnp.int32, (8, 2 * RANK), 1) < RANK
    for d in range(32):
        b0, v0 = 8 * (d % 2), 8 * (d % 4 // 2)
        b = total[32 + d // 2, b0 : b0 + 8]
        v = total[48 + d // 4, v0 : v0 + 8]
        if d % 2 == 0:
            v = pltpu.roll(v, RANK, 1)
        both[0, d, 0:8] = total[d, 0:8]
        both[0, d, 8:16] = jnp.where(left, b, v)
        both[1, d, 0:8] = total[d, 8:16]
        both[1, d, 8:16] = jnp.where(left, pltpu.roll(b, RANK, 1), 0.0)
    margin = ride_of(total[56])
    margin_out[...] = jnp.broadcast_to(margin, (8, 2 * RANK))
    keep[...] = both[h]
    send[0:32] = both[1 - h].astype(BF)
    send[32] = split3(margin)


def scale_kernel(keep, met, margin_in, scaled, margin_out):
    margin = margin_in[0:1, 0:1] + ride_of(met[32].astype(F32))
    margin_out[...] = jnp.broadcast_to(margin, (8, 2 * RANK))
    weight = -BETA / (1.0 + jnp.exp(BETA * margin))
    scaled[...] = ((keep[...] + met[0:32].astype(F32)) * weight[None]).astype(BF)


def sum_kernel(shares, spread):
    total = shares[0].astype(F32)
    for q in range(1, 32):
        total = total + shares[q].astype(F32)
    for q in range(8):
        spread[q] = total


def finish_kernel(total, a_q, b_q, a_v, b_v):
    for e in range(8):
        at = slice(8 * e, 8 * e + 8)
        a_q[at, :] = total[e, 0:8, 0:RANK]
        a_v[at, :] = total[e, 0:8, RANK : 2 * RANK]
        b_q[at, :] = total[e, 8:16, 0:RANK]
    for q in range(2):
        b_v[8 * q : 8 * q + 8, :] = total[2 * q, 8:16, RANK : 2 * RANK]


def small_call(kernel, out_shape, *args, scalars=0, scratch=()):
    vm = pl.BlockSpec(memory_space=pltpu.VMEM)
    return pl.pallas_call(
        kernel,
        out_shape=out_shape,
        in_specs=[pl.BlockSpec(memory_space=pltpu.SMEM)] * scalars + [vm] * (len(args) - scalars),
        out_specs=(vm,) * len(out_shape),
        scratch_shapes=scratch,
        compiler_params=pltpu.CompilerParams(vmem_limit_bytes=16 * 2**20),
    )(*args)


def pack_kernel(h_ref, wq, wk, wv, wo, aq, av, bq, bv, hidden, gain, out, xn, thin, thin_v, flat, hid, sems, out_sem):
    hid_copy = pltpu.make_async_copy(hidden, hid, sems.at[6])
    hid_copy.start()

    def fetch(parts):
        copies = [pltpu.make_async_copy(src, dst, sems.at[n]) for n, (src, dst) in enumerate(parts)]
        for copy in copies:
            copy.start()
        return copies

    @pl.when(h_ref[0] == 0)
    def _():
        small = [(aq, thin.at[0]), (av, thin.at[1]), (bq, thin.at[2]), (bv, thin_v)]
        copies = fetch(small + [(wq, flat.at[:, 256:2304]), (wo.at[:, 0:384], flat.at[:, 2304:2688])])
        for copy in copies[:4]:
            copy.wait()
        for n in range(3):
            flat[:, n * RANK : n * RANK + RANK] = thin[n]
        flat[:, 3 * RANK : 4 * RANK] = jnp.zeros((TOK, RANK), BF)
        flat[0:16, 3 * RANK : 4 * RANK] = thin_v[...]
        for copy in copies[4:]:
            copy.wait()

    @pl.when(h_ref[0] == 1)
    def _():
        for copy in fetch([(wk, flat.at[:, 0:512]), (wv, flat.at[:, 512:1024]), (wo.at[:, 384:2048], flat.at[:, 1024:2688])]):
            copy.wait()

    done = pltpu.make_async_copy(flat, out, out_sem)
    done.start()
    hid_copy.wait()
    x = hid[...].astype(F32)
    xn[...] = (x * lax.rsqrt(jnp.mean(x * x, axis=-1, keepdims=True) + EPS) * gain[...]).astype(BF)
    done.wait()


def pack(*args):
    vm, anyspace = pl.BlockSpec(memory_space=pltpu.VMEM), pl.BlockSpec(memory_space=pl.ANY)
    return pl.pallas_call(
        pack_kernel,
        out_shape=(jax.ShapeDtypeStruct((TOK, 2688), BF), jax.ShapeDtypeStruct((ROWS, D), BF)),
        in_specs=[pl.BlockSpec(memory_space=pltpu.SMEM)] + [anyspace] * 9 + [vm],
        out_specs=(anyspace, vm),
        scratch_shapes=[
            pltpu.VMEM((3, TOK, RANK), BF), pltpu.VMEM((16, RANK), BF), pltpu.VMEM((TOK, 2688), BF), pltpu.VMEM((ROWS, D), BF),
            pltpu.SemaphoreType.DMA((7,)), pltpu.SemaphoreType.DMA,
        ],
        compiler_params=pltpu.CompilerParams(vmem_limit_bytes=60 * 2**20),
    )(*args)


def local_step(own_block, full, xa, kc, ks, bias, hid, ans, gain, sign):
    vm, anyspace = pl.BlockSpec(memory_space=pltpu.VMEM), pl.BlockSpec(memory_space=pl.ANY)
    bf, f32 = (lambda *s: pltpu.VMEM(s, BF)), (lambda *s: pltpu.VMEM(s, F32))
    return pl.pallas_call(
        local_kernel,
        out_shape=jax.ShapeDtypeStruct((4, 57, 16, 2 * RANK), BF),
        in_specs=[pl.BlockSpec(memory_space=pltpu.SMEM), anyspace] + [vm] * 8,
        out_specs=vm,
        scratch_shapes=[
            bf(D, 256), bf(D, 2 * KVW), bf(D, D), bf(D, D),
            bf(ALL, 2 * RANK), bf(KVW, 2 * RANK),
            bf(PARTS, L, HD), bf(PARTS, L, HD), bf(PARTS, L, HD),
            bf(2, PARTS, QROWS, HD), f32(PARTS, QROWS, L), bf(PARTS, QROWS, L), f32(PARTS, QROWS, HD),
            bf(2 * ROWS, D), f32(ROWS, D), bf(ROWS, D), bf(PARTS, QROWS, HD), bf(ROWS, D), bf(ALL, KVW), bf(ALL, 2 * RANK),
            pltpu.SemaphoreType.DMA((6, PIECES)),
        ],
        compiler_params=pltpu.CompilerParams(vmem_limit_bytes=50 * 2**20),
        cost_estimate=pl.CostEstimate(flops=24_000_000_000, bytes_accessed=27_000_000, transcendentals=2_100_000),
    )(own_block, full, xa, kc, ks, bias, hid, ans, gain, sign)


def body(hidden, answer_rows, resp_mask, attn_gain, final_gain, w_query, w_key, w_value, w_out, a_query, b_query, a_value, b_value):
    hidden = hidden[0]
    y_pos, h_pos = lax.axis_index("y"), lax.axis_index("h")

    h_one = jnp.full((1,), 1, jnp.int32) * h_pos
    packed, xn = pack(
        h_one, w_query, w_key, w_value, w_out, a_query, a_value, b_query, b_value, hidden.reshape(ROWS, D), attn_gain.reshape(1, D)
    )
    other = lax.ppermute(xn, "h", [(0, 1), (1, 0)])
    full = lax.all_gather(packed, ("h",) + OWN, axis=0, tiled=True).reshape(2, D, packed.shape[1])

    two = jnp.concatenate([xn, other], axis=0)
    every = lax.all_to_all(jnp.broadcast_to(two[None], (4,) + two.shape), "y", 0, 0, tiled=True)
    xa = every.reshape(ALL, D)

    block = jnp.arange(BLOCKS, dtype=jnp.int32)
    source = (block // 2) * 2 + jnp.bitwise_xor(block % 2, h_pos)
    token = jnp.arange(TOK, dtype=jnp.int32)
    key_pos = source[:, None] * TOK + token[None, :]
    own_pos = (y_pos * 2 + h_pos) * TOK + token
    frequency = THETA ** (-(jnp.arange(HD // 2, dtype=F32) * 2.0) / HD)
    row_pos = jnp.broadcast_to(key_pos[:, None, :], (BLOCKS, 2, TOK)).reshape(ALL)
    angles = row_pos.astype(F32)[:, None] * frequency[None, :]
    cosine, sine = jnp.cos(angles), jnp.sin(angles)
    kc = jnp.concatenate([cosine, cosine], axis=1)
    ks = jnp.concatenate([-sine, sine], axis=1)
    bias = jnp.where(own_pos[:, None] >= key_pos.reshape(1, L), 0.0, -1e30).astype(F32)
    sign = (resp_mask[0].astype(F32) * jnp.array([1.0, -1.0], F32)[:, None]).reshape(ROWS, 1)
    own_block = jnp.full((1,), 2, jnp.int32) * y_pos

    mine = local_step(own_block, full, xa, kc, ks, bias, hidden.reshape(ROWS, D), answer_rows.reshape(ROWS, D), final_gain.reshape(1, D), sign)

    got = lax.all_to_all(mine, "y", 0, 0, tiled=True)
    tile, vector = (16, 2 * RANK), jax.ShapeDtypeStruct((8, 2 * RANK), F32)
    keep, send, part = small_call(
        halves_kernel, (jax.ShapeDtypeStruct((32,) + tile, F32), jax.ShapeDtypeStruct((33,) + tile, BF), vector), h_one, got, scalars=1,
        scratch=(pltpu.VMEM((2, 32) + tile, F32),),
    )
    met = lax.ppermute(send, "h", [(0, 1), (1, 0)])
    scaled, margin = small_call(scale_kernel, (jax.ShapeDtypeStruct((32,) + tile, BF), vector), keep, met, part)
    shares = lax.all_to_all(scaled, OWN, 0, 0, tiled=True)
    loss = jax.nn.softplus(-BETA * margin[0, :1])
    (spread,) = small_call(sum_kernel, (jax.ShapeDtypeStruct((8,) + tile, F32),), shares)
    total = lax.all_to_all(spread, ("y", "h"), 0, 0, tiled=True)
    square = jax.ShapeDtypeStruct((TOK, RANK), F32)
    grads = small_call(finish_kernel, (square, square, square, jax.ShapeDtypeStruct((16, RANK), F32)), total)
    return tuple(grads) + (loss,)


def solution(mesh):
    fine = Mesh(mesh.devices.reshape(4, 2, 4, 2, 4), AXES)
    seq = ("y", "h")
    weights = P(OWN, None)
    in_specs = (P(OWN, None, seq, None), P(OWN, None, seq, None), P(OWN, None, seq), P(), P()) + (weights,) * 8
    out_specs = (weights,) * 4 + (P(OWN),)
    return jax.shard_map(body, mesh=fine, in_specs=in_specs, out_specs=out_specs, check_vma=False)
```
